32 devices in a mesh: leaf: 8 (over z, x), rows: 4 (over y, core).
Axes of the slice: x: 2, y: 2, z: 4, core: 2. Of those that a mesh axis runs over, the one named last changes fastest.
Arguments:
- loads_first: bfloat16 [49152, 256], P(('leaf', 'rows')), may hold values from -6 to 6
- loads_second: bfloat16 [24576, 256], P(('leaf', 'rows')), may hold values from -6 to 6
- loads_third: bfloat16 [12288, 256], P(('leaf', 'rows')), may hold values from -6 to 6
- loads_fourth: bfloat16 [6144, 256], P(('leaf', 'rows')), may hold values from -6 to 6
- inverse_first: bfloat16 [49152, 6144], P(('leaf', 'rows')), as said below
- inverse_second: bfloat16 [24576, 6144], P(('leaf', 'rows')), as said below
- inverse_third: bfloat16 [12288, 6144], P(('leaf', 'rows')), as said below
- inverse_fourth: bfloat16 [6144, 6144], P(('leaf', 'rows')), as said below
- panel_first: bfloat16 [1536, 49152], P(None, ('leaf', 'rows')), may hold values from -0.078125 to 0.078125
- panel_second: bfloat16 [1536, 24576], P(None, ('leaf', 'rows')), may hold values from -0.078125 to 0.078125
- panel_third: bfloat16 [1536, 12288], P(None, ('leaf', 'rows')), may hold values from -0.078125 to 0.078125
- panel_fourth: bfloat16 [1536, 6144], P(None, ('leaf', 'rows')), may hold values from -0.078125 to 0.078125
- blocks_first: int32 [8, 12], replicated, may hold values from 0 to 47, as said below
- blocks_second: int32 [4, 12], replicated, may hold values from 0 to 47, as said below
- blocks_third: int32 [2, 12], replicated, may hold values from 0 to 47, as said below
Outputs:
- solved_first: bfloat16 [49152, 256], P(('leaf', 'rows'))
- solved_second: bfloat16 [24576, 256], P(('leaf', 'rows'))
- solved_third: bfloat16 [12288, 256], P(('leaf', 'rows'))
- solved_fourth: bfloat16 [6144, 256], P(('leaf', 'rows'))
- ancestor_update: float32 [1536, 256], P(('leaf', 'rows'))
The draws below stay inside these ranges and needn't reach their ends.
Inputs may be any that keep to these rules, and one draw needn't show every extreme that they name: `blocks_first`: each row lists 12 distinct block numbers in increasing order. `blocks_second`: each row lists 12 distinct block numbers in increasing order. `blocks_third`: each row lists 12 distinct block numbers in increasing order. `inverse_first`: each block of 6144 rows is lower triangular with a positive diagonal. `inverse_second`: each block of 6144 rows is lower triangular with a positive diagonal. `inverse_third`: each block of 6144 rows is lower triangular with a positive diagonal. `inverse_fourth`: each block of 6144 rows is lower triangular with a positive diagonal.
All inputs are finite; a program needn't handle non-finite values.
Results may differ from the reference program's by a relative error of at most 0.015.
Values may be sent and summed in bfloat16 or wider, within the bound.
No kernel may reach another device: no remote copies, remote signals or barrier semaphores. Data moves between devices by JAX's collectives and lax.ppermute only.
A program may use at most 128 MiB of HBM per device.

```python
import jax
import jax.numpy as jnp
from jax import lax

S = 6144
NRHS = 256
UR = 1536
BLK = 128
NSN0 = 8
NSN1 = 4
NSN2 = 2
NSN3 = 1
SB = 48
UB = 12


def draw_inverse(key, node_total):

    def draw_node(node_index):
        node_key = jax.random.fold_in(key, node_index)
        noise_key, diag_key = jax.random.split(node_key)
        noise = jax.random.normal(noise_key, (S, S), jnp.float32)
        diagonal = jax.random.uniform(diag_key, (S, 1), jnp.float32, 0.5, 1.5)
        row_ids = lax.broadcasted_iota(jnp.int32, (S, S), 0)
        col_ids = lax.broadcasted_iota(jnp.int32, (S, S), 1)
        lower_part = jnp.where(row_ids > col_ids, noise * S ** (-0.5), 0.0)
        return jnp.where(row_ids == col_ids, diagonal, lower_part)
    stacked = lax.map(draw_node, jnp.arange(node_total, dtype=jnp.int32))
    return stacked.reshape(node_total * S, S)


def draw_table(key, node_total):
    key_list = jax.random.split(jax.random.fold_in(key, 7), node_total)

    def draw_row(row_key):
        return jnp.sort(jax.random.permutation(row_key, S // BLK)[:UR // BLK])
    picked = jax.vmap(draw_row)(key_list).astype(jnp.int32)
    picked = picked.at[0, 0].set(0)
    picked = picked.at[0, UR // BLK - 1].set(S // BLK - 1)
    return picked


def draw_inverse_first(key, part):
    return draw_inverse(key, NSN0).astype(jnp.bfloat16)


def draw_inverse_second(key, part):
    return draw_inverse(key, NSN1).astype(jnp.bfloat16)


def draw_inverse_third(key, part):
    return draw_inverse(key, NSN2).astype(jnp.bfloat16)


def draw_inverse_fourth(key, part):
    return draw_inverse(key, NSN3).astype(jnp.bfloat16)


def draw_blocks_first(key, part):
    return draw_table(key, NSN0)


def draw_blocks_second(key, part):
    return draw_table(key, NSN1)


def draw_blocks_third(key, part):
    return draw_table(key, NSN2)


def level_of(own_key, dims, cuts, least, high):
    def one(position, shards_of):
        draws = jax.random.uniform(jax.random.fold_in(jax.random.fold_in(own_key, 6), position), (shards_of,), jnp.float32, least / len(cuts), high / len(cuts))
        return jnp.repeat(jnp.exp(draws), dims[position] // shards_of).reshape((-1,) + (1,) * (len(dims) - position - 1))

    loudness = one(*cuts[0])
    for cut in cuts[1:]:
        loudness = loudness * one(*cut)
    return loudness


def scatter_about(key, shape, width, most, shards=(), kind=jnp.bfloat16):
    gain = level_of(key, shape, shards, -0.22, 0.18) if shards else 1.0
    values = jax.random.normal(key, shape, jnp.float32) * width * gain
    return jnp.minimum(jnp.maximum(values, -most), most).astype(kind)


def setup_inputs(seed: int = 0) -> dict:
    key_of = jax.random.split(jax.random.key(seed), 16)
    return {
        "loads_first": scatter_about(key_of[0], (NSN0 * S, NRHS), 1.0, 6.0, ((0, 32),)),
        "loads_second": scatter_about(key_of[1], (NSN1 * S, NRHS), 1.0, 6.0, ((0, 32),)),
        "loads_third": scatter_about(key_of[2], (NSN2 * S, NRHS), 1.0, 6.0, ((0, 32),)),
        "loads_fourth": scatter_about(key_of[3], (NSN3 * S, NRHS), 1.0, 6.0, ((0, 32),)),
        "inverse_first": draw_inverse_first(jax.random.fold_in(key_of[15], 71), 0),
        "inverse_second": draw_inverse_second(jax.random.fold_in(key_of[15], 71), 0),
        "inverse_third": draw_inverse_third(jax.random.fold_in(key_of[15], 71), 0),
        "inverse_fourth": draw_inverse_fourth(jax.random.fold_in(key_of[15], 71), 0),
        "panel_first": scatter_about(key_of[8], (UR, NSN0 * S), S ** -0.5, 0.078125, ((1, 32),)),
        "panel_second": scatter_about(key_of[9], (UR, NSN1 * S), S ** -0.5, 0.078125, ((1, 32),)),
        "panel_third": scatter_about(key_of[10], (UR, NSN2 * S), S ** -0.5, 0.078125, ((1, 32),)),
        "panel_fourth": scatter_about(key_of[11], (UR, NSN3 * S), S ** -0.5, 0.078125, ((1, 32),)),
        "blocks_first": draw_blocks_first(jax.random.fold_in(key_of[15], 71), 0),
        "blocks_second": draw_blocks_second(jax.random.fold_in(key_of[15], 71), 0),
        "blocks_third": draw_blocks_third(jax.random.fold_in(key_of[15], 71), 0),
    }


def place_rows(update, table_row):
    blocks = update.reshape(UB, BLK, NRHS)
    spread = jnp.zeros((SB, BLK, NRHS), jnp.float32).at[table_row].add(blocks)
    return spread.reshape(S, NRHS)


def reference(loads_first, loads_second, loads_third, loads_fourth, inverse_first, inverse_second, inverse_third, inverse_fourth, panel_first, panel_second, panel_third, panel_fourth, blocks_first, blocks_second, blocks_third):
    load_list = [loads_first, loads_second, loads_third, loads_fourth]
    inverse_list = [inverse_first, inverse_second, inverse_third, inverse_fourth]
    panel_list = [panel_first, panel_second, panel_third, panel_fourth]
    table_list = [blocks_first, blocks_second, blocks_third]
    node_counts = [NSN0, NSN1, NSN2, NSN3]
    solved_levels = []
    previous = []
    for level_index in range(4):
        solved_blocks = []
        updates = []
        for node_index in range(node_counts[level_index]):
            load_block = load_list[level_index][node_index * S:(node_index + 1) * S]
            if level_index == 0:
                prepared = load_block
            else:
                row_table = table_list[level_index - 1]
                assembled = load_block.astype(jnp.float32) - place_rows(previous[2 * node_index], row_table[2 * node_index]) - place_rows(previous[2 * node_index + 1], row_table[2 * node_index + 1])
                prepared = assembled.astype(jnp.bfloat16)
            inverse_block = inverse_list[level_index][node_index * S:(node_index + 1) * S]
            solved = jnp.dot(inverse_block, prepared, preferred_element_type=jnp.float32).astype(jnp.bfloat16)
            solved_blocks.append(solved)
            panel_block = panel_list[level_index][:, node_index * S:(node_index + 1) * S]
            updates.append(jnp.dot(panel_block, solved, preferred_element_type=jnp.float32))
        solved_levels.append(jnp.concatenate(solved_blocks, 0))
        previous = updates
    ancestor_update = jnp.concatenate(previous, 0)
    return (solved_levels[0], solved_levels[1], solved_levels[2], solved_levels[3], ancestor_update)
```

```python
import functools

import jax
import jax.numpy as jnp
from jax import lax
from jax.experimental import pallas as pl
from jax.experimental.pallas import tpu as pltpu
from jax.sharding import Mesh
from jax.sharding import PartitionSpec as P

BF16 = jnp.bfloat16
F32 = jnp.float32
AXES = ("hi", "z2", "z1", "x", "rows")
VMEM = pl.BlockSpec(memory_space=pltpu.VMEM)
SMEM = pl.BlockSpec(memory_space=pltpu.SMEM)
MIB = 1 << 20


def permute(value, mask, upward=0):
    total = lax.axis_size(AXES)
    pairs = [(i, i ^ mask) for i in range(total) if not upward or (i ^ mask) > i]
    return lax.ppermute(value, AXES, pairs)


def in_vmem(value):
    return pltpu.with_memory_space_constraint(value, pltpu.VMEM)


def row_tile(rows):
    return next(t for t in (512, 384, 256, 192, 128, 96, 64, 48, 32, 16) if rows % t == 0)


def call(kernel, outs, scalars, operands, scratch=(), limit=24, flops=0):
    return pl.pallas_call(
        kernel,
        out_shape=[pltpu.VMEM(o.shape, o.dtype) for o in outs],
        in_specs=[SMEM] + [VMEM] * len(operands),
        out_specs=[VMEM] * len(outs),
        scratch_shapes=list(scratch),
        compiler_params=pltpu.CompilerParams(vmem_limit_bytes=limit * MIB),
        cost_estimate=pl.CostEstimate(
            flops=flops,
            bytes_accessed=sum(o.size * o.dtype.itemsize for o in operands),
            transcendentals=0,
        ),
    )(scalars, *[in_vmem(o) for o in operands])


def piece_kernel(has_acc, scalars, a0, a1, b0, b1, *rest):
    out = rest[-1]
    total = jnp.dot(a0[...], b0[...], preferred_element_type=F32)
    total += jnp.dot(a1[...], b1[...], preferred_element_type=F32)
    if has_acc:
        total += rest[0][...]
    out[...] = total.astype(out.dtype)


def add_pieces(inverse, columns, b0, b1, acc, out_dtype):
    rows, depth = inverse.shape[0], b0.shape[0]
    cols = b0.shape[1]
    tile = row_tile(rows)
    whole = pl.BlockSpec((depth, cols), lambda i, s: (0, 0))
    block = pl.BlockSpec((tile, cols), lambda i, s: (i, 0))
    specs = [
        pl.BlockSpec((tile, depth), lambda i, s: (i, s[0])),
        pl.BlockSpec((tile, depth), lambda i, s: (i, s[1])),
        whole,
        whole,
    ]
    operands = [inverse, inverse, b0, b1]
    if acc is not None:
        specs.append(block)
        operands.append(acc)
    return pl.pallas_call(
        functools.partial(piece_kernel, acc is not None),
        out_shape=jax.ShapeDtypeStruct((rows, cols), out_dtype),
        grid_spec=pltpu.PrefetchScalarGridSpec(
            num_scalar_prefetch=1, grid=(rows // tile,), in_specs=specs, out_specs=block
        ),
        compiler_params=pltpu.CompilerParams(vmem_limit_bytes=24 * MIB),
        cost_estimate=pl.CostEstimate(
            flops=4 * rows * depth * cols, bytes_accessed=4 * rows * depth, transcendentals=0
        ),
    )(columns, *operands)


def split_panel(core, panel, x_ref, keep, send):
    rows, half = keep.shape
    tile = row_tile(rows)

    def step(i, carry):
        at = pl.ds(pl.multiple_of(i * tile, tile), tile)
        part = jnp.dot(panel[at, :], x_ref[...], preferred_element_type=F32)
        low, high = part[:, :half], part[:, half:]
        keep[at, :] = jnp.where(core == 0, low, high)
        send[at, :] = jnp.where(core == 0, high, low).astype(BF16)
        return carry

    lax.fori_loop(0, rows // tile, step, 0)


def panel_kernel(scalars, panel, x_ref, keep, send):
    split_panel(scalars[0], panel, x_ref, keep, send)


def first_sum_kernel(chunk, scalars, keep, received, own, *sends):
    for mask in range(len(sends) + 1):
        at = pl.ds(pl.multiple_of((scalars[1] ^ mask) * chunk, chunk), chunk)
        total = keep[at, :] + received[at, :].astype(F32)
        if mask == 0:
            own[...] = total
        else:
            sends[mask - 1][...] = total.astype(BF16)


def second_sum_kernel(scalars, own, *rest):
    total = own[...]
    for other in rest[:-1]:
        total += other[...].astype(F32)
    rest[-1][...] = total.astype(rest[-1].dtype)


def reduce_plane(keep, send, scalars, masks):
    received = permute(send, 1)
    chunk, half = keep.shape[0] // len(masks), keep.shape[1]
    shapes = [jax.ShapeDtypeStruct((chunk, half), F32)]
    shapes += [jax.ShapeDtypeStruct((chunk, half), BF16)] * (len(masks) - 1)
    own, *sends = call(
        functools.partial(first_sum_kernel, chunk), shapes, scalars, [keep, received]
    )
    arrived = [permute(value, mask) for value, mask in zip(sends, masks[1:])]
    return call(
        second_sum_kernel,
        [jax.ShapeDtypeStruct((chunk, half), BF16)],
        scalars,
        [own, *arrived],
    )[0]


def select_kernel(rows_blocks, width, table, source, target, sems):
    copies = []
    for i in range(rows_blocks):
        at = pl.multiple_of(table[i] * width, width)
        copies.append(
            pltpu.make_async_copy(
                source.at[:, pl.ds(at, width)],
                target.at[:, pl.ds(i * width, width)],
                sems.at[i],
            )
        )
    for copy in copies:
        copy.start()
    for copy in copies:
        copy.wait()


def select_columns(inverse, table, width):
    count = table.shape[0]
    return pl.pallas_call(
        functools.partial(select_kernel, count, width),
        out_shape=jax.ShapeDtypeStruct((inverse.shape[0], count * width), BF16),
        in_specs=[SMEM, pl.BlockSpec(memory_space=pl.ANY)],
        out_specs=pl.BlockSpec(memory_space=pl.ANY),
        scratch_shapes=[pltpu.SemaphoreType.DMA((count,))],
    )(table, inverse)


def level_kernel(slots, split, scalars, *refs):
    count = len(slots)
    pieces, (picked, base, panel) = refs[: 2 * count], refs[2 * count : 2 * count + 3]
    outs = refs[2 * count + 3 : -2]
    update, x_ref = refs[-2:]
    core, place = scalars[0], scalars[1]
    chunk, half = pieces[0].shape
    child = update.shape[0] // 2
    for j, (slot, mask) in enumerate(slots):
        at = pl.multiple_of(slot * child + (place ^ mask) * chunk, 16)
        update[pl.ds(at, chunk), :half] = pieces[2 * j][...]
        update[pl.ds(at, chunk), half:] = pieces[2 * j + 1][...]
    rows = picked.shape[0]
    tile = row_tile(rows)

    def step(i, carry):
        at = pl.ds(pl.multiple_of(i * tile, tile), tile)
        part = jnp.dot(picked[at, :], update[...], preferred_element_type=F32)
        low, high = part[:, :half], part[:, half:]
        x_low = base[at, :half] - jnp.where(core == 0, low, high)
        x_high = base[at, half:] - jnp.where(core == 0, high, low)
        outs[0][at, :half] = x_low.astype(BF16)
        outs[0][at, half:] = x_high.astype(BF16)
        return carry

    lax.fori_loop(0, rows // tile, step, 0)
    if split:
        split_panel(core, panel, outs[0], outs[1], outs[2])
    else:
        tile = row_tile(panel.shape[0])

        def panel_step(i, carry):
            at = pl.ds(pl.multiple_of(i * tile, tile), tile)
            outs[1][at, :] = jnp.dot(panel[at, :], outs[0][...], preferred_element_type=F32)
            return carry

        lax.fori_loop(0, panel.shape[0] // tile, panel_step, 0)


def solve_level(pieces, slots, scalars, picked, base, panel, split):
    rows, cols = base.shape
    total = panel.shape[0]
    outs = [jax.ShapeDtypeStruct((rows, cols), BF16)]
    if split:
        outs += [
            jax.ShapeDtypeStruct((total, cols // 2), F32),
            jax.ShapeDtypeStruct((total, cols // 2), BF16),
        ]
    else:
        outs.append(jax.ShapeDtypeStruct((total, cols), F32))
    return call(
        functools.partial(level_kernel, slots, split),
        outs,
        scalars,
        [*pieces, picked, base, panel],
        scratch=[pltpu.VMEM((picked.shape[1], cols), BF16), pltpu.VMEM((8, 128), F32)],
        flops=2 * cols * (picked.size + panel.size),
    )


def in_order(bit, own, other):
    return jnp.where(
        bit == 0, jnp.concatenate([own, other], 0), jnp.concatenate([other, own], 0)
    )


def per_device(
    loads_first,
    loads_second,
    loads_third,
    loads_fourth,
    inverse_first,
    inverse_second,
    inverse_third,
    inverse_fourth,
    panel_first,
    panel_second,
    panel_third,
    panel_fourth,
    blocks_first,
    blocks_second,
    blocks_third,
):
    n_rows = lax.axis_size("rows")
    n_y = n_rows // 2
    row_index = lax.axis_index("rows")
    core, y_index = row_index & 1, row_index >> 1
    x_index, z1, z2 = (lax.axis_index(a) for a in ("x", "z1", "z2"))
    leaf = ((lax.axis_index("hi") * 2 + z2) * 2 + z1) * 2 + x_index
    mask_x, mask_z1, mask_z2 = n_rows, 2 * n_rows, 4 * n_rows
    plane = [x * mask_x + y * 2 for x in range(2) for y in range(n_y)]
    plane_index = x_index * n_y + y_index
    column = [y * 2 for y in range(n_y)]
    by_column = jnp.stack([core, y_index]).astype(jnp.int32)
    by_plane = jnp.stack([core, plane_index]).astype(jnp.int32)
    update_rows = panel_first.shape[0]
    width = update_rows // blocks_first.shape[1]

    def gather_plane(value):
        return lax.all_gather(value, ("x", "rows"), axis=0, tiled=True)

    all_second = gather_plane(loads_second)
    pair_third = in_order(z1, loads_third, permute(loads_third, mask_z1))
    low = in_order(z1, loads_fourth, permute(loads_fourth, mask_z1))
    high = in_order(z1, permute(loads_fourth, mask_z2), permute(loads_fourth, mask_z2 | mask_z1))
    quad_fourth = in_order(z2, low, high)

    def by_z(value, count):
        rows, cols = value.shape
        each = rows // (2 * n_rows * count)
        split = value.reshape(2 * n_rows, count, each, cols)
        return split.transpose(1, 0, 2, 3).reshape(rows, cols)

    all_third = by_z(gather_plane(pair_third), 2)
    all_fourth = by_z(gather_plane(quad_fourth), 4)
    bases = [
        jnp.dot(inverse, loads, preferred_element_type=F32)
        for inverse, loads in (
            (inverse_second, all_second),
            (inverse_third, all_third),
            (inverse_fourth, all_fourth),
        )
    ]
    picked = []
    for level, (inverse, table) in enumerate(
        (
            (inverse_second, blocks_first),
            (inverse_third, blocks_second),
            (inverse_fourth, blocks_third),
        )
    ):
        child = leaf >> level
        rows = [lax.dynamic_index_in_dim(table, c, 0, keepdims=False) for c in (child, child ^ 1)]
        picked.append(select_columns(inverse, jnp.concatenate(rows), width))

    sibling = permute(loads_first, 1)
    acc = None
    for mask in column:
        if mask == 0:
            b0, b1 = loads_first, sibling
        else:
            b0 = permute(loads_first, mask, upward=1)
            b1 = permute(b0, 1)
        places = jnp.stack([row_index ^ mask, row_index ^ mask ^ 1]).astype(jnp.int32)
        last = mask == column[-1]
        acc = add_pieces(inverse_first, places, b0, b1, acc, BF16 if last else F32)
    solved_first = acc
    half = solved_first.shape[1] // 2
    keep, send = call(
        panel_kernel,
        [
            jax.ShapeDtypeStruct((update_rows, half), F32),
            jax.ShapeDtypeStruct((update_rows, half), BF16),
        ],
        by_column,
        [panel_first, solved_first],
        flops=2 * panel_first.size * 2 * half,
    )
    part = reduce_plane(keep, send, by_column, column)
    pieces, slots = [], []
    for mask in plane:
        piece = part if mask == 0 else permute(part, mask)
        pieces += [piece, permute(piece, 1)]
        slots.append((mask // mask_x, (mask % mask_x) // 2))

    solved_second, keep, send = solve_level(
        pieces, slots, by_column, picked[0], bases[0], panel_second, True
    )
    part = reduce_plane(keep, send, by_plane, plane)

    def spread(own, sib):
        pieces, slots = [], []
        for slot, value in ((0, own), (1, sib)):
            for place, mask in enumerate(plane):
                piece = value if mask == 0 else permute(value, mask)
                pieces += [piece, permute(piece, 1)]
                slots.append((slot, place))
        return pieces, slots

    pieces, slots = spread(part, permute(part, mask_z1))

    solved_third, keep, send = solve_level(
        pieces, slots, by_plane, picked[1], bases[1], panel_third, True
    )
    part = reduce_plane(keep, send, by_plane, plane)
    part = (part.astype(F32) + permute(part, mask_z1).astype(F32)).astype(BF16)
    pieces, slots = spread(part, permute(part, mask_z2))

    solved_fourth, total = solve_level(
        pieces, slots, by_plane, picked[2], bases[2], panel_fourth, False
    )
    each = update_rows // (8 * n_rows)
    cols = total.shape[1]

    def pick(value, index):
        return lax.dynamic_index_in_dim(value, index, 0, keepdims=False)

    total = total.reshape(4, 2 * n_y, 2, each, cols)
    keep = lax.dynamic_index_in_dim(total, core, 2, keepdims=False)
    send = lax.dynamic_index_in_dim(total, core ^ 1, 2, keepdims=False)
    total = keep + permute(send.astype(BF16), 1).astype(F32)
    own = lax.dynamic_index_in_dim(total, plane_index, 1, keepdims=False)
    for place, mask in enumerate(plane[1:], 1):
        value = lax.dynamic_index_in_dim(total, plane_index ^ place, 1, keepdims=False)
        own = own + permute(value.astype(BF16), mask).astype(F32)
    z_index = z2 * 2 + z1
    ancestor = pick(own, z_index)
    for m in range(1, 4):
        value = pick(own, z_index ^ m).astype(BF16)
        ancestor = ancestor + permute(value, m * mask_z1).astype(F32)
    return solved_first, solved_second, solved_third, solved_fourth, ancestor


def solution(mesh):
    n_leaf, n_rows = mesh.shape["leaf"], mesh.shape["rows"]
    fine = Mesh(mesh.devices.reshape(n_leaf // 8, 2, 2, 2, n_rows), AXES)
    rows, cols = P(AXES, None), P(None, AXES)
    return jax.shard_map(
        per_device,
        mesh=fine,
        in_specs=(rows,) * 8 + (cols,) * 4 + (P(),) * 3,
        out_specs=(rows,) * 5,
        check_vma=False,
    )
```

```python
import functools
import math

import jax
import jax.numpy as jnp
from jax import lax
from jax.experimental import pallas as pl
from jax.experimental.pallas import tpu as pltpu
from jax.sharding import Mesh
from jax.sharding import PartitionSpec as P

BF16 = jnp.bfloat16
F32 = jnp.float32
AXES = ("hi", "z2", "z1", "x", "y", "core")
PLANE = ("x", "y")
VMEM = pl.BlockSpec(memory_space=pltpu.VMEM)
SMEM = pl.BlockSpec(memory_space=pltpu.SMEM)
MIB = 1 << 20


def permute(value, mask, upward=False):
    total = lax.axis_size(AXES)
    pairs = [(i, i ^ mask) for i in range(total) if not upward or (i ^ mask) > i]
    return lax.ppermute(value, AXES, pairs)


def row_tile(rows):
    return next(t for t in (512, 384, 256, 192, 128, 96, 64, 48, 32, 16) if rows % t == 0)


def aval(rows, cols, dtype):
    return jax.ShapeDtypeStruct((rows, cols), dtype)


def call(kernel, outs, scalars, operands, scratch=(), limit=12, flops=0):
    operands = [pltpu.with_memory_space_constraint(o, pltpu.VMEM) for o in operands]
    return pl.pallas_call(
        kernel,
        out_shape=[pltpu.VMEM(o.shape, o.dtype) for o in outs],
        in_specs=[SMEM] + [VMEM] * len(operands),
        out_specs=[VMEM] * len(outs),
        scratch_shapes=list(scratch),
        compiler_params=pltpu.CompilerParams(vmem_limit_bytes=limit * MIB),
        cost_estimate=pl.CostEstimate(
            flops=flops,
            bytes_accessed=sum(o.size * o.dtype.itemsize for o in operands),
            transcendentals=0,
        ),
    )(scalars, *operands)


def tiles(rows, step):
    tile = row_tile(rows)

    def body(i, carry):
        step(pl.ds(pl.multiple_of(i * tile, tile), tile))
        return carry

    lax.fori_loop(0, rows // tile, body, 0)


def dot(a, b):
    return jnp.dot(a, b, preferred_element_type=F32)


def piece_kernel(scalars, inverse, b0, b1, *rest):
    out, depth = rest[-1], b0.shape[0]
    at0 = pl.ds(pl.multiple_of(scalars[1] * depth, depth), depth)
    at1 = pl.ds(pl.multiple_of(scalars[2] * depth, depth), depth)

    def step(at):
        total = dot(inverse[at, at0], b0[...]) + dot(inverse[at, at1], b1[...])
        if len(rest) > 1:
            total += rest[0][at, :]
        out[at, :] = total

    tiles(inverse.shape[0], step)


def last_piece_kernel(scalars, inverse, b0, b1, acc, panel, out, keep, send):
    depth = b0.shape[0]
    at0 = pl.ds(pl.multiple_of(scalars[1] * depth, depth), depth)
    at1 = pl.ds(pl.multiple_of(scalars[2] * depth, depth), depth)

    def step(at):
        total = acc[at, :] + dot(inverse[at, at0], b0[...])
        out[at, :] = (total + dot(inverse[at, at1], b1[...])).astype(BF16)

    tiles(inverse.shape[0], step)
    split_panel(scalars[0], panel, out, keep, send)


def split_panel(core, panel, x_ref, keep, send):
    half = keep.shape[1]

    def step(at):
        part = dot(panel[at, :], x_ref[...])
        low, high = part[:, :half], part[:, half:]
        keep[at, :] = jnp.where(core == 0, low, high)
        send[at, :] = jnp.where(core == 0, high, low).astype(BF16)

    tiles(panel.shape[0], step)


def pair_sum_kernel(scalars, keep, received, out):
    out[...] = (keep[...] + received[...].astype(F32)).astype(out.dtype)


def chunk_sum_kernel(count, scalars, chunks, out):
    rows = out.shape[0]
    total = chunks[:rows, :].astype(F32)
    for i in range(1, count):
        total += chunks[i * rows : (i + 1) * rows, :].astype(F32)
    out[...] = total.astype(out.dtype)


def reduce_over(value, axes, scalars, dtype):
    count = lax.axis_size(axes)
    arrived = lax.all_to_all(value, axes, 0, 0, tiled=True)
    rows, cols = value.shape
    return call(
        functools.partial(chunk_sum_kernel, count),
        [aval(rows // count, cols, dtype)],
        scalars,
        [arrived],
    )[0]


def pair_sum(keep, send, scalars):
    received = permute(send, 1)
    return call(pair_sum_kernel, [aval(*keep.shape, BF16)], scalars, [keep, received])[0]


def level_kernel(places, unit, last, scalars, table, mine, other, loads, inverse, panel, *rest):
    solved, keep, send, ready = rest[:4]
    core, half, width = scalars[0], mine.shape[1], table.shape[1]
    block = panel.shape[0] // width
    ready[...] = loads[...]
    for i, (child, index, row) in enumerate(places):
        at = pl.multiple_of(table[child, index] * block + row, unit)
        a = mine[i * unit : (i + 1) * unit, :].astype(F32)
        b = other[i * unit : (i + 1) * unit, :].astype(F32)
        low = ready[pl.ds(at, unit), :half].astype(F32) - jnp.where(core == 0, a, b)
        high = ready[pl.ds(at, unit), half:].astype(F32) - jnp.where(core == 0, b, a)
        ready[pl.ds(at, unit), :half] = low.astype(BF16)
        ready[pl.ds(at, unit), half:] = high.astype(BF16)

    def step(at):
        solved[at, :] = dot(inverse[at, :], ready[...]).astype(BF16)

    tiles(inverse.shape[0], step)
    if not last:
        split_panel(core, panel, solved, keep, send)
        return
    total, outgoing = rest[4:]

    def panel_step(at):
        total[at, :] = dot(panel[at, :], solved[...])

    tiles(panel.shape[0], panel_step)
    each = keep.shape[0] // (4 * last)
    for z in range(4):
        for place in range(last):
            source = (z * last + place) * 2
            at = pl.ds((place * 4 + z) * each, each)
            keep[at, :] = total[pl.ds(pl.multiple_of((source + core) * each, 8), each), :]
            outgoing[at, :] = total[pl.ds(pl.multiple_of((source + 1 - core) * each, 8), each), :]
    send[...] = outgoing[...].astype(BF16)


def solve_level(table, places, unit, scalars, mine, other, loads, inverse, panel, last=0):
    rows, cols = inverse.shape[0], loads.shape[1]
    total = panel.shape[0]
    shape = (total // 2, cols) if last else (total, cols // 2)
    scratch = [pltpu.VMEM(loads.shape, BF16)]
    if last:
        scratch += [pltpu.VMEM((total, cols), F32), pltpu.VMEM(shape, F32)]

    def kernel(scalars, *refs):
        level_kernel(places, unit, last, scalars, *refs)

    operands = [mine, other, loads, inverse, panel]
    operands = [pltpu.with_memory_space_constraint(o, pltpu.VMEM) for o in operands]
    outs = [aval(rows, cols, BF16), aval(*shape, F32), aval(*shape, BF16)]
    return pl.pallas_call(
        kernel,
        out_shape=[pltpu.VMEM(o.shape, o.dtype) for o in outs],
        in_specs=[SMEM, SMEM] + [VMEM] * len(operands),
        out_specs=[VMEM] * len(outs),
        scratch_shapes=scratch,
        compiler_params=pltpu.CompilerParams(vmem_limit_bytes=16 * MIB),
        cost_estimate=pl.CostEstimate(
            flops=2 * cols * (inverse.size + panel.size),
            bytes_accessed=2 * (inverse.size + panel.size),
            transcendentals=0,
        ),
    )(scalars, table, *operands)


def in_order(bit, own, other):
    return jnp.where(
        bit == 0, jnp.concatenate([own, other], 0), jnp.concatenate([other, own], 0)
    )


def per_device(
    loads_first,
    loads_second,
    loads_third,
    loads_fourth,
    inverse_first,
    inverse_second,
    inverse_third,
    inverse_fourth,
    panel_first,
    panel_second,
    panel_third,
    panel_fourth,
    blocks_first,
    blocks_second,
    blocks_third,
):
    n_y, n_rows = lax.axis_size("y"), 2 * lax.axis_size("y")
    core, x_index, z1, z2 = (lax.axis_index(a) for a in ("core", "x", "z1", "z2"))
    row_index = lax.axis_index("y") * 2 + core
    leaf = ((lax.axis_index("hi") * 2 + z2) * 2 + z1) * 2 + x_index
    mask_z1, mask_z2 = 2 * n_rows, 4 * n_rows
    cores = core[None].astype(jnp.int32)
    update_rows = panel_first.shape[0]
    block = update_rows // blocks_first.shape[1]
    cols = loads_first.shape[1]
    half = cols // 2

    sibling = permute(loads_first, 1)
    acc = None
    arrived = [(0, loads_first, sibling)]
    for y in range(1, n_y):
        piece = permute(loads_first, 2 * y, upward=True)
        arrived.append((2 * y, piece, permute(piece, 1)))
    for mask, b0, b1 in arrived[:-1]:
        scalars = jnp.stack([core, row_index ^ mask, row_index ^ mask ^ 1]).astype(jnp.int32)
        operands = [inverse_first, b0, b1] + ([acc] if mask else [])
        acc = call(
            piece_kernel,
            [aval(inverse_first.shape[0], cols, F32)],
            scalars,
            operands,
            flops=4 * inverse_first.shape[0] * b0.size,
        )[0]

    loads_third, loads_fourth, acc = lax.optimization_barrier((loads_third, loads_fourth, acc))

    def gather_plane(value):
        return lax.all_gather(value, ("x", "y", "core"), axis=0, tiled=True)

    def by_z(value, count):
        rows = value.shape[0]
        split = value.reshape(2 * n_rows, count, rows // (2 * n_rows * count), cols)
        return split.transpose(1, 0, 2, 3).reshape(rows, cols)

    all_second = gather_plane(loads_second)
    pair_third = in_order(z1, loads_third, permute(loads_third, mask_z1))
    low = in_order(z1, loads_fourth, permute(loads_fourth, mask_z1))
    high = in_order(z1, permute(loads_fourth, mask_z2), permute(loads_fourth, mask_z2 | mask_z1))
    quad_fourth = in_order(z2, low, high)
    all_third = by_z(gather_plane(pair_third), 2)
    all_fourth = by_z(gather_plane(quad_fourth), 4)

    mask, b0, b1 = arrived[-1]
    scalars = jnp.stack([core, row_index ^ mask, row_index ^ mask ^ 1]).astype(jnp.int32)
    solved_first, keep, send = call(
        last_piece_kernel,
        [
            aval(inverse_first.shape[0], cols, BF16),
            aval(update_rows, half, F32),
            aval(update_rows, half, BF16),
        ],
        scalars,
        [inverse_first, b0, b1, acc, panel_first],
        flops=4 * inverse_first.shape[0] * b0.size + 2 * panel_first.size * cols,
    )
    part = reduce_over(pair_sum(keep, send, cores), "y", cores, BF16)

    def spread(value):
        mine = lax.all_gather(value, PLANE, axis=0, tiled=True)
        return mine, permute(mine, 1)

    def both_tables(table, level):
        child = leaf >> level
        return jnp.stack(
            [lax.dynamic_index_in_dim(table, c, 0, keepdims=False) for c in (child, child ^ 1)]
        )

    mine, other = spread(part)
    chunk = part.shape[0]
    unit = math.gcd(chunk, block)
    places = []
    for row in range(0, 2 * update_rows, unit):
        child, row = divmod(row, update_rows)
        places.append((child, row // block, row % block))
    first_two = blocks_first.reshape(-1, 2, blocks_first.shape[1])
    table = lax.dynamic_index_in_dim(first_two, leaf >> 1, 0, keepdims=False)
    solved_second, keep, send = solve_level(
        table, places, unit, cores, mine, other, all_second, inverse_second, panel_second
    )
    part = reduce_over(pair_sum(keep, send, cores), PLANE, cores, BF16)

    chunk = part.shape[0]
    unit = math.gcd(chunk, block)
    places = []
    for place in range(2 * n_y):
        for child in range(2):
            for row in range(place * chunk, (place + 1) * chunk, unit):
                places.append((child, row // block, row % block))

    mine, other = spread(jnp.concatenate([part, permute(part, mask_z1)], 0))
    solved_third, keep, send = solve_level(
        both_tables(blocks_second, 1),
        places,
        unit,
        cores,
        mine,
        other,
        all_third,
        inverse_third,
        panel_third,
    )
    part = reduce_over(pair_sum(keep, send, cores), PLANE, cores, BF16)
    part = (part.astype(F32) + permute(part, mask_z1).astype(F32)).astype(BF16)
    mine, other = spread(jnp.concatenate([part, permute(part, mask_z2)], 0))
    solved_fourth, keep, send = solve_level(
        both_tables(blocks_third, 2),
        places,
        unit,
        cores,
        mine,
        other,
        all_fourth,
        inverse_fourth,
        panel_fourth,
        last=2 * n_y,
    )
    part = reduce_over(pair_sum(keep, send, cores), PLANE, cores, F32)
    parts = part.reshape(4, -1, cols)
    z_index = z2 * 2 + z1
    ancestor = lax.dynamic_index_in_dim(parts, z_index, 0, keepdims=False)
    for m in range(1, 4):
        value = lax.dynamic_index_in_dim(parts, z_index ^ m, 0, keepdims=False)
        ancestor = ancestor + permute(value.astype(BF16), m * mask_z1).astype(F32)
    return solved_first, solved_second, solved_third, solved_fourth, ancestor


def solution(mesh):
    n_leaf, n_rows = mesh.shape["leaf"], mesh.shape["rows"]
    fine = Mesh(mesh.devices.reshape(n_leaf // 8, 2, 2, 2, n_rows // 2, 2), AXES)
    rows, cols = P(AXES, None), P(None, AXES)
    return jax.shard_map(
        per_device,
        mesh=fine,
        in_specs=(rows,) * 8 + (cols,) * 4 + (P(),) * 3,
        out_specs=(rows,) * 5,
        check_vma=False,
    )
```

```python
import functools
import math

import jax
import jax.numpy as jnp
from jax import lax
from jax.experimental import pallas as pl
from jax.experimental.pallas import tpu as pltpu
from jax.sharding import Mesh
from jax.sharding import PartitionSpec as P

BF16 = jnp.bfloat16
F32 = jnp.float32
AXES = ("hi", "z2", "z1", "x", "y", "core")
PLANE = ("x", "y")
VMEM = pl.BlockSpec(memory_space=pltpu.VMEM)
SMEM = pl.BlockSpec(memory_space=pltpu.SMEM)
ANY = pl.BlockSpec(memory_space=pl.ANY)
MIB = 1 << 20


def permute(value, mask, upward=False):
    total = lax.axis_size(AXES)
    pairs = [(i, i ^ mask) for i in range(total) if not upward or (i ^ mask) > i]
    return lax.ppermute(value, AXES, pairs)


def row_tile(rows):
    return next(t for t in (512, 384, 256, 192, 128, 96, 64, 48, 32, 16) if rows % t == 0)


def aval(rows, cols, dtype):
    return jax.ShapeDtypeStruct((rows, cols), dtype)


def kernel_call(kernel, outs, scalars, vmem, hbm=(), scratch=(), limit=8, pin=True):
    operands = [pltpu.with_memory_space_constraint(o, pltpu.VMEM) if pin else o for o in vmem]
    return pl.pallas_call(
        kernel,
        out_shape=[pltpu.VMEM(o.shape, o.dtype) if inside else o for o, inside in outs],
        in_specs=[SMEM] + [VMEM] * len(vmem) + [ANY] * len(hbm),
        out_specs=[VMEM if inside else ANY for _, inside in outs],
        scratch_shapes=list(scratch),
        compiler_params=pltpu.CompilerParams(vmem_limit_bytes=limit * MIB),
        cost_estimate=pl.CostEstimate(flops=0, bytes_accessed=0, transcendentals=0),
    )(scalars, *operands, *[pltpu.with_memory_space_constraint(o, pltpu.HBM) for o in hbm])


def tiles(rows, step):
    tile = row_tile(rows)

    def body(i, carry):
        step(pl.ds(pl.multiple_of(i * tile, tile), tile))
        return carry

    lax.fori_loop(0, rows // tile, body, 0)


def dot(a, b):
    return jnp.dot(a, b, preferred_element_type=F32)


def start_all(sources, targets, sems):
    copies = [
        pltpu.make_async_copy(source, target, sems.at[i])
        for i, (source, target) in enumerate(zip(sources, targets))
    ]
    for copy in copies:
        copy.start()
    return copies


def near_kernel(scalars, b0, b1, inverse, panel, acc, far, panel_out, near, sems):
    rows, depth = inverse.shape[0], b0.shape[0]
    tile = row_tile(rows)
    n_far = far.shape[1] // depth
    columns = [
        pl.ds(pl.multiple_of(scalars[1 + i] * depth, depth), depth) for i in range(2 + n_far)
    ]
    sources, targets = [], []
    for i in range(rows // tile):
        at = pl.ds(i * tile, tile)
        for j in range(2):
            sources.append(inverse.at[at, columns[j]])
            targets.append(near.at[at, pl.ds(j * depth, depth)])
    for j in range(n_far):
        sources.append(inverse.at[:, columns[2 + j]])
        targets.append(far.at[:, pl.ds(j * depth, depth)])
    sources.append(panel)
    targets.append(panel_out)
    copies = start_all(sources, targets, sems)
    for i in range(rows // tile):
        at = pl.ds(i * tile, tile)
        copies[2 * i].wait()
        copies[2 * i + 1].wait()
        acc[at, :] = dot(near[at, :depth], b0[...]) + dot(near[at, depth:], b1[...])
    for copy in copies[2 * (rows // tile) :]:
        copy.wait()


def far_kernel(n_far, scalars, acc, panel, far, *refs):
    pieces, (solved, keep, send, x_ref, sem) = refs[:n_far], refs[n_far:]
    depth = pieces[0].shape[0]
    core, half = scalars[0], keep.shape[1]

    def step(at):
        total = acc[at, :]
        for j, piece in enumerate(pieces):
            total += dot(far[at, j * depth : (j + 1) * depth], piece[...])
        x_ref[at, :] = total.astype(BF16)

    tiles(far.shape[0], step)
    result = pltpu.make_async_copy(x_ref, solved, sem)
    result.start()

    def panel_step(at):
        part = dot(panel[at, :], x_ref[...])
        low, high = part[:, :half], part[:, half:]
        keep[at, :] = jnp.where(core == 0, low, high)
        send[at, :] = jnp.where(core == 0, high, low).astype(BF16)

    tiles(panel.shape[0], panel_step)
    result.wait()


def split_kernel(scalars, *refs):
    *arrays, keep, send = refs
    core, half, first = scalars[0], keep.shape[1], 0
    for array in arrays:
        at = pl.ds(first, array.shape[0])
        first += array.shape[0]
        low, high = array[:, :half], array[:, half:]
        keep[at, :] = jnp.where(core == 0, low, high)
        send[at, :] = jnp.where(core == 0, high, low)


def pack_kernel(scalars, keep, received, *outs):
    first = 0
    for out in outs:
        rows = out.shape[0] // 2
        out[:rows, :] = keep[pl.ds(first, rows), :]
        out[rows:, :] = received[pl.ds(first, rows), :]
        first += rows


def join_columns(core, own, other):
    return jnp.where(
        core == 0, jnp.concatenate([own, other], 1), jnp.concatenate([other, own], 1)
    )


def pair_sum_kernel(scalars, keep, received, out):
    out[...] = (keep[...] + received[...].astype(F32)).astype(out.dtype)


def chunk_sum_kernel(count, scalars, chunks, out):
    rows = out.shape[0]
    total = chunks[:rows, :].astype(F32)
    for i in range(1, count):
        total += chunks[i * rows : (i + 1) * rows, :].astype(F32)
    out[...] = total.astype(out.dtype)


def reduce_over(value, axes, scalars, dtype):
    count = lax.axis_size(axes)
    arrived = lax.all_to_all(value, axes, 0, 0, tiled=True)
    rows, cols = value.shape
    return kernel_call(
        functools.partial(chunk_sum_kernel, count),
        [(aval(rows // count, cols, dtype), True)],
        scalars,
        [arrived],
    )[0]


def z_split_kernel(at_z, scalars, value, own, *sends):
    rows = own.shape[0]
    for mask in range(4):
        at = pl.ds(pl.multiple_of((scalars[at_z] ^ mask) * rows, rows), rows)
        if mask == 0:
            own[...] = value[at, :]
        else:
            sends[mask - 1][...] = value[at, :].astype(BF16)


def z_sum_kernel(scalars, own, a, b, c, keep, send, total):
    total[...] = own[...] + a[...].astype(F32) + b[...].astype(F32) + c[...].astype(F32)
    rows = keep.shape[0]
    keep[...] = total[pl.ds(pl.multiple_of(scalars[0] * rows, 8), rows), :]
    send[...] = total[pl.ds(pl.multiple_of((1 - scalars[0]) * rows, 8), rows), :]


def level_kernel(plan, scalars, mine, *refs):
    unit, places, block, at_table, at_order, size, n_pieces, plane = plan
    sources, refs = refs[:4], refs[4:]
    pieces, refs = refs[:n_pieces], refs[n_pieces:]
    update, x_keep, x_send, ready, *held = refs[:8]
    sems, part_sems, *spare = refs[8:]
    rows = x_keep.shape[0]
    tile = min(192, row_tile(rows))
    count = rows // tile

    def fetch(which, i):
        at = pl.ds(pl.multiple_of(i * tile, tile), tile)
        return pltpu.make_async_copy(
            sources[which].at[at, :], held[which].at[at, :], part_sems.at[which * count + i]
        )

    def fetch_panel(which):
        return pltpu.make_async_copy(
            sources[2 + which], held[2 + which], part_sems.at[2 * count + which]
        )

    runs, targets = [], []
    for piece in pieces:
        for row in range(0, piece.shape[0], size):
            at = pl.multiple_of(scalars[at_order + len(runs)] * size, size)
            runs.append(piece.at[pl.ds(row, size), :])
            targets.append(ready.at[pl.ds(at, size), :])
    copies = start_all(runs, targets, sems)
    for which in range(2):
        fetch(which, 0).start()
    for copy in copies:
        copy.wait()
    for i, (index, row) in enumerate(places):
        at = pl.ds(pl.multiple_of(scalars[at_table + index] * block + row, unit), unit)
        value = mine[i * unit : (i + 1) * unit, :].astype(F32)
        ready[at, :] = (ready[at, :].astype(F32) - value).astype(BF16)

    def step(i, carry):
        at = pl.ds(pl.multiple_of(i * tile, tile), tile)
        for which, out in ((0, x_keep), (1, x_send)):
            fetch(which, i).wait()

            @pl.when(i + 1 < count)
            def _():
                fetch(which, i + 1).start()

            @pl.when(i + 1 == count)
            def _():
                fetch_panel(which).start()

            out[at, :] = dot(held[which][at, :], ready[...]).astype(BF16)
        return carry

    lax.fori_loop(0, count, step, 0)
    panel_a, panel_b = held[2:]
    for which in range(2):
        fetch_panel(which).wait()
    if not plane:

        def panel_step(at):
            part = dot(panel_a[at, :], x_keep[...]) + dot(panel_b[at, :], x_send[...])
            update[at, :] = part.astype(BF16)

        tiles(update.shape[0], panel_step)
        return
    total = spare[0]

    def last_step(at):
        dims = (((0,), (0,)), ((), ()))
        part = lax.dot_general(panel_a[:, at], x_keep[...], dims, preferred_element_type=F32)
        part += lax.dot_general(panel_b[:, at], x_send[...], dims, preferred_element_type=F32)
        total[at, :] = part.astype(BF16)

    tiles(update.shape[0], last_step)
    each = update.shape[0] // (4 * plane)
    for z in range(4):
        for place in range(plane):
            source = (z * plane + place) * each
            target = (place * 4 + z) * each
            update[target : target + each, :] = total[source : source + each, :]


def solve_level(scalars, plan, mine, inverses, panels, pieces, update_rows):
    rows, depth = inverses[0].shape
    half, size, plane = mine.shape[1], plan[5], plan[7]
    count = rows // min(192, row_tile(rows))
    scratch = [pltpu.VMEM((depth, half), BF16)]
    scratch += [pltpu.VMEM(v.shape, BF16) for v in (*inverses, *panels)]
    scratch += [pltpu.SemaphoreType.DMA((depth // size,)), pltpu.SemaphoreType.DMA((2 * count + 2,))]
    if plane:
        scratch.append(pltpu.VMEM((update_rows, half), BF16))
    outs = [(aval(r, half, BF16), True) for r in (update_rows, rows, rows)]
    return kernel_call(
        functools.partial(level_kernel, plan),
        outs,
        scalars,
        [mine],
        [*inverses, *panels, *pieces],
        scratch,
        limit=34,
    )


def per_device(
    loads_first,
    loads_second,
    loads_third,
    loads_fourth,
    inverse_first,
    inverse_second,
    inverse_third,
    inverse_fourth,
    panel_first,
    panel_second,
    panel_third,
    panel_fourth,
    blocks_first,
    blocks_second,
    blocks_third,
):
    n_y, n_rows = lax.axis_size("y"), 2 * lax.axis_size("y")
    core, x_index, y_index = (lax.axis_index(a) for a in ("core", "x", "y"))
    z1, z2 = lax.axis_index("z1"), lax.axis_index("z2")
    row_index = y_index * 2 + core
    z_index = z2 * 2 + z1
    leaf = (lax.axis_index("hi") * 4 + z_index) * 2 + x_index
    mask_x, mask_z1, mask_z2 = n_rows, 2 * n_rows, 4 * n_rows
    y_masks = [2 * y for y in range(1, n_y)]
    plane_masks = [(x, y) for y in range(n_y) for x in range(2)]
    update_rows, width = panel_first.shape[0], blocks_first.shape[1]
    block = update_rows // width
    rows, depth = inverse_first.shape[0], loads_first.shape[0]
    cols = loads_first.shape[1]
    half = cols // 2

    values = [core, row_index, row_index ^ 1]
    for mask in y_masks:
        values += [row_index ^ mask, row_index ^ mask ^ 1]
    at_z = len(values)
    values.append(z_index)
    at_order = []
    for planes in ([0], [z1, z1 ^ 1], [z_index, z_index ^ 2, z_index ^ 1, z_index ^ 3]):
        at_order.append(len(values))
        for x, y in plane_masks:
            place = ((x_index ^ x) * n_y + (y_index ^ y)) * 2
            for z in planes:
                values += [z * 2 * n_rows + place + (core ^ other) for other in range(2)]
    at_table = [len(values) + 2 * width * i for i in range(3)]
    children = [(leaf >> 1) * 2, (leaf >> 1) * 2 + 1]
    parts = [jnp.stack([jnp.asarray(v, jnp.int32) for v in values])]
    for table, pair in (
        (blocks_first, children),
        (blocks_second, [leaf >> 1, (leaf >> 1) ^ 1]),
        (blocks_third, [leaf >> 2, (leaf >> 2) ^ 1]),
    ):
        parts += [lax.dynamic_index_in_dim(table, c, 0, keepdims=False) for c in pair]
    scalars = jnp.concatenate(parts)
    scalars, loads_second, loads_third, loads_fourth = lax.optimization_barrier(
        (scalars, loads_second, loads_third, loads_fourth)
    )

    tie = lax.optimization_barrier

    n_far = 2 * len(y_masks)
    sibling = permute(loads_first, 1)
    shards = [permute(loads_first, mask, upward=True) for mask in y_masks]
    loads = [loads_second, loads_third, loads_fourth]
    sizes = [v.shape[0] for v in loads]
    keep, send = kernel_call(
        split_kernel, [(aval(sum(sizes), half, BF16), True)] * 2, scalars, loads, pin=False
    )
    received = permute(send, 1)
    keep, received, inverse_third, panel_third = tie((keep, received, inverse_third, panel_third))
    across_third = permute(inverse_third, 1), permute(panel_third, 1)
    acc, far, panel = kernel_call(
        near_kernel,
        [
            (aval(rows, cols, F32), True),
            (aval(rows, n_far * depth, BF16), True),
            (aval(*panel_first.shape, BF16), True),
        ],
        scalars,
        [loads_first, sibling],
        [inverse_first, panel_first],
        [
            pltpu.VMEM((rows, 2 * depth), BF16),
            pltpu.SemaphoreType.DMA((2 * (rows // row_tile(rows)) + n_far + 1,)),
        ],
        limit=16,
    )
    own_second, half_third, half_fourth = kernel_call(
        pack_kernel, [(aval(2 * s, half, BF16), True) for s in sizes], scalars, [keep, received]
    )
    x_second = permute(own_second, mask_x)
    z1_third = permute(half_third, mask_z1)
    z2_fourth = permute(half_fourth, mask_z2)
    shards, acc, own_second, x_second, z1_third, z2_fourth, across_third, panel_second = tie(
        (shards, acc, own_second, x_second, z1_third, z2_fourth, across_third, panel_second)
    )

    pieces = [v for shard in shards for v in (shard, permute(shard, 1))]
    pieces, panel_second = tie((pieces, panel_second))
    across_panel = permute(panel_second, 1)
    own_third = jnp.concatenate([half_third, z1_third], 0)
    half_fourth = jnp.concatenate([half_fourth, z2_fourth], 0)
    z1_fourth = permute(half_fourth, mask_z1)
    y_second = [permute(own_second, mask) for mask in y_masks]
    x_third = permute(own_third, mask_x)
    solved_first, keep, send = kernel_call(
        functools.partial(far_kernel, n_far),
        [
            (aval(rows, cols, BF16), False),
            (aval(update_rows, half, F32), True),
            (aval(update_rows, half, BF16), True),
        ],
        scalars,
        [acc, panel, far, *pieces],
        [],
        [pltpu.VMEM((rows, cols), BF16), pltpu.SemaphoreType.DMA],
    )
    keep, send, x_third, across_panel = tie((keep, send, x_third, across_panel))
    received = permute(send, 1)
    update = kernel_call(
        pair_sum_kernel, [(aval(*keep.shape, BF16), True)], scalars, [keep, received]
    )[0]
    update, y_second, z1_fourth, inverse_second = tie(
        (update, y_second, z1_fourth, inverse_second)
    )

    def with_x(x_piece, own, y_pieces):
        pieces = [own, x_piece]
        for piece in y_pieces:
            pieces += [piece, permute(piece, mask_x)]
        return pieces

    inverses = [(inverse_second, permute(inverse_second, 1))]
    panels = [(panel_second, across_panel), (panel_third, across_third[1])]
    inverses.append((inverse_third, across_third[0]))
    pieces_second = with_x(x_second, own_second, y_second)
    own_fourth = jnp.concatenate([half_fourth, z1_fourth], 0)
    part = reduce_over(update, "y", scalars, BF16)
    part, pieces_second, own_fourth = tie((part, pieces_second, own_fourth))

    def spread(value):
        return lax.all_gather(value, PLANE, axis=0, tiled=True)

    def plan_of(level, chunk, both):
        unit = math.gcd(chunk, block)
        places = []
        for place in range(2 * n_y):
            for child in range(2) if both else [place // n_y]:
                start = (place if both else place % n_y) * chunk
                for row in range(start, start + chunk, unit):
                    places.append((child * width + row // block, row % block))
        last = 2 * n_y if level == 2 else 0
        pieces = len(plane_masks)
        return (
            unit, places, block, at_table[level], at_order[level], sizes[level], pieces, last,
        )

    mine = spread(part)
    mine, own_third, own_fourth = tie((mine, own_third, own_fourth))
    y_third = [permute(own_third, mask) for mask in y_masks]
    x_fourth = permute(own_fourth, mask_x)
    update, keep, send = solve_level(
        scalars,
        plan_of(0, part.shape[0], False),
        mine,
        inverses[0],
        panels[0],
        pieces_second,
        update_rows,
    )
    update, y_third, x_fourth, keep, send, inverse_fourth, panel_fourth = tie(
        (update, y_third, x_fourth, keep, send, inverse_fourth, panel_fourth)
    )
    panel_fourth = panel_fourth.T
    inverses.append((inverse_fourth, permute(inverse_fourth, 1)))
    panels.append((panel_fourth, permute(panel_fourth, 1)))

    part = reduce_over(update, PLANE, scalars, BF16)
    part, y_third, own_fourth, keep, send = tie((part, y_third, own_fourth, keep, send))
    sibling = permute(part, mask_z1)
    pieces_third = with_x(x_third, own_third, y_third)
    y_fourth = [permute(own_fourth, mask) for mask in y_masks]
    solved_second = join_columns(core, keep, permute(send, 1))
    part, sibling, pieces_third, y_fourth, solved_second, inverses, panels = tie(
        (part, sibling, pieces_third, y_fourth, solved_second, inverses, panels)
    )
    mine = spread(jnp.concatenate([part, sibling], 0))
    update, keep, send = solve_level(
        scalars,
        plan_of(1, part.shape[0], True),
        mine,
        inverses[1],
        panels[1],
        pieces_third,
        update_rows,
    )

    part = reduce_over(update, PLANE, scalars, BF16)
    part, y_fourth, keep, send = tie((part, y_fourth, keep, send))
    pieces_fourth = with_x(x_fourth, own_fourth, y_fourth)
    solved_third = join_columns(core, keep, permute(send, 1))
    part = (part.astype(F32) + permute(part, mask_z1).astype(F32)).astype(BF16)
    sibling = permute(part, mask_z2)
    part, sibling, pieces_fourth, solved_third = tie((part, sibling, pieces_fourth, solved_third))
    mine = spread(jnp.concatenate([part, sibling], 0))
    update, keep_fourth, send_fourth = solve_level(
        scalars,
        plan_of(2, part.shape[0], True),
        mine,
        inverses[2],
        panels[2],
        pieces_fourth,
        update_rows,
    )
    solved_fourth = join_columns(core, keep_fourth, permute(send_fourth, 1))
    part = reduce_over(update, PLANE, scalars, F32)
    chunk = part.shape[0] // 4
    own, *sends = kernel_call(
        functools.partial(z_split_kernel, at_z),
        [(aval(chunk, half, F32), True)] + [(aval(chunk, half, BF16), True)] * 3,
        scalars,
        [part],
    )
    arrived = [permute(value, (i + 1) * mask_z1) for i, value in enumerate(sends)]
    keep, send = kernel_call(
        z_sum_kernel,
        [(aval(chunk // 2, half, F32), True)] * 2,
        scalars,
        [own, *arrived],
        scratch=[pltpu.VMEM((chunk, half), F32)],
    )
    ancestor = join_columns(core, keep, permute(send, 1))
    return solved_first, solved_second, solved_third, solved_fourth, ancestor


def solution(mesh):
    n_leaf, n_rows = mesh.shape["leaf"], mesh.shape["rows"]
    fine = Mesh(mesh.devices.reshape(n_leaf // 8, 2, 2, 2, n_rows // 2, 2), AXES)
    rows, cols = P(AXES, None), P(None, AXES)
    return jax.shard_map(
        per_device,
        mesh=fine,
        in_specs=(rows,) * 8 + (cols,) * 4 + (P(),) * 3,
        out_specs=(rows,) * 5,
        check_vma=False,
    )
```

```python
import functools
import math

import jax
import jax.numpy as jnp
from jax import lax
from jax.experimental import pallas as pl
from jax.experimental.pallas import tpu as pltpu
from jax.sharding import Mesh
from jax.sharding import PartitionSpec as P

BF16 = jnp.bfloat16
F32 = jnp.float32
AXES = ("hi", "z2", "z1", "x", "y", "core")
PLANE = ("x", "y")
VMEM = pl.BlockSpec(memory_space=pltpu.VMEM)
SMEM = pl.BlockSpec(memory_space=pltpu.SMEM)
ANY = pl.BlockSpec(memory_space=pl.ANY)
MIB = 1 << 20


def permute(value, mask, upward=False):
    total = lax.axis_size(AXES)
    pairs = [(i, i ^ mask) for i in range(total) if not upward or (i ^ mask) > i]
    return lax.ppermute(value, AXES, pairs)


def row_tile(rows):
    return next(t for t in (512, 384, 256, 192, 128, 96, 64, 48, 32, 16) if rows % t == 0)


def aval(rows, cols, dtype):
    return jax.ShapeDtypeStruct((rows, cols), dtype)


def kernel_call(kernel, outs, scalars, vmem, hbm=(), scratch=(), limit=8):
    operands = [pltpu.with_memory_space_constraint(o, pltpu.VMEM) for o in vmem]
    return pl.pallas_call(
        kernel,
        out_shape=[pltpu.VMEM(o.shape, o.dtype) if inside else o for o, inside in outs],
        in_specs=[SMEM] + [VMEM] * len(vmem) + [ANY] * len(hbm),
        out_specs=[ANY if inside is False else VMEM for _, inside in outs],
        scratch_shapes=list(scratch),
        compiler_params=pltpu.CompilerParams(vmem_limit_bytes=limit * MIB),
        cost_estimate=pl.CostEstimate(flops=1, bytes_accessed=1, transcendentals=0),
    )(scalars, *operands, *[pltpu.with_memory_space_constraint(o, pltpu.HBM) for o in hbm])


def tiles(rows, step):
    tile = row_tile(rows)

    def body(i, carry):
        step(pl.ds(pl.multiple_of(i * tile, tile), tile))
        return carry

    lax.fori_loop(0, rows // tile, body, 0)


def dot(a, b):
    return jnp.dot(a, b, preferred_element_type=F32)


def start_all(sources, targets, sems):
    copies = [
        pltpu.make_async_copy(source, target, sems.at[i])
        for i, (source, target) in enumerate(zip(sources, targets))
    ]
    for copy in copies:
        copy.start()
    return copies


def near_kernel(scalars, b0, b1, inverse, panel, acc, far, panel_out, near, sems):
    rows, depth = inverse.shape[0], b0.shape[0]
    tile = row_tile(rows)
    n_far = far.shape[1] // depth
    columns = [
        pl.ds(pl.multiple_of(scalars[1 + i] * depth, depth), depth) for i in range(2 + n_far)
    ]
    sources, targets = [], []
    for i in range(rows // tile):
        at = pl.ds(i * tile, tile)
        for j in range(2):
            sources.append(inverse.at[at, columns[j]])
            targets.append(near.at[at, pl.ds(j * depth, depth)])
    for j in range(n_far):
        sources.append(inverse.at[:, columns[2 + j]])
        targets.append(far.at[:, pl.ds(j * depth, depth)])
    sources.append(panel)
    targets.append(panel_out)
    copies = start_all(sources, targets, sems)
    for i in range(rows // tile):
        at = pl.ds(i * tile, tile)
        copies[2 * i].wait()
        copies[2 * i + 1].wait()
        acc[at, :] = dot(near[at, :depth], b0[...]) + dot(near[at, depth:], b1[...])
    for copy in copies[2 * (rows // tile) :]:
        copy.wait()


def split_panel(core, panel, x_ref, keep, send):
    half = keep.shape[1]

    def step(at):
        part = dot(panel[at, :], x_ref[...])
        low, high = part[:, :half], part[:, half:]
        keep[at, :] = jnp.where(core == 0, low, high)
        send[at, :] = jnp.where(core == 0, high, low).astype(BF16)

    tiles(panel.shape[0], step)


def far_kernel(n_far, n_next, scalars, acc, panel, far, *refs):
    pieces, refs = refs[:n_far], refs[n_far:]
    solved, keep, send = refs[n_next : n_next + 3]
    x_ref, sem, sems = refs[-3:]
    copies = start_all(refs[:n_next], refs[n_next + 3 : -3], sems)
    depth = pieces[0].shape[0]

    def step(at):
        total = acc[at, :]
        for j, piece in enumerate(pieces):
            total += dot(far[at, j * depth : (j + 1) * depth], piece[...])
        x_ref[at, :] = total.astype(BF16)

    tiles(far.shape[0], step)
    result = pltpu.make_async_copy(x_ref, solved, sem)
    result.start()
    split_panel(scalars[0], panel, x_ref, keep, send)
    for copy in [*copies, result]:
        copy.wait()


def split_kernel(scalars, *refs):
    *arrays, keep, send, held, sems = refs
    core, half, first, targets = scalars[0], keep.shape[1], 0, []
    for array in arrays:
        targets.append(held.at[pl.ds(first, array.shape[0]), :])
        first += array.shape[0]
    for copy in start_all(arrays, targets, sems):
        copy.wait()
    low, high = held[:, :half], held[:, half:]
    keep[...] = jnp.where(core == 0, low, high)
    send[...] = jnp.where(core == 0, high, low)


def pack_kernel(groups, scalars, keep, received, *outs):
    for group, out in zip(groups, outs):
        at = 0
        for first, rows in group:
            out[at : at + rows, :] = keep[first : first + rows, :]
            out[at + rows : at + 2 * rows, :] = received[first : first + rows, :]
            at += 2 * rows


def join_kernel(scalars, own, other, out):
    half = own.shape[1]
    out[:, :half] = jnp.where(scalars[0] == 0, own[...], other[...])
    out[:, half:] = jnp.where(scalars[0] == 0, other[...], own[...])


def join_columns(scalars, own, other):
    rows, half = own.shape
    return kernel_call(join_kernel, [(aval(rows, 2 * half, own.dtype), None)], scalars, [own, other])[0]


def hand_out(place, value, own, sends):
    rows = own.shape[0]
    for mask, out in enumerate([own, *sends]):
        at = pl.ds(pl.multiple_of((place ^ mask) * rows, rows), rows)
        out[...] = value[at, :].astype(out.dtype)


def pair_sum_kernel(at_place, scalars, keep, received, own, *rest):
    *sends, total = rest
    total[...] = keep[...] + received[...].astype(F32)
    hand_out(scalars[at_place], total, own, sends)


def sum_kernel(scalars, own, *rest):
    total = own[...]
    for other in rest[:-1]:
        total += other[...].astype(F32)
    rest[-1][...] = total.astype(rest[-1].dtype)


def chunks_of(rows, cols, masks):
    rows //= len(masks)
    return [(aval(rows, cols, F32), True)] + [(aval(rows, cols, BF16), True)] * (len(masks) - 1)


def pair_sum(keep, send, scalars, at_place, masks):
    received = permute(send, 1)
    return kernel_call(
        functools.partial(pair_sum_kernel, at_place),
        chunks_of(*keep.shape, masks),
        scalars,
        [keep, received],
        scratch=[pltpu.VMEM(keep.shape, F32)],
    )


def reduce_chunks(chunks, masks, scalars):
    own, *sends = chunks
    arrived = [permute(value, mask) for value, mask in zip(sends, masks[1:])]
    return kernel_call(
        sum_kernel, [(aval(*own.shape, BF16), True)], scalars, [own, *arrived]
    )[0]


def core_split_kernel(count, scalars, chunks, keep, send, total):
    rows = total.shape[0]
    value = chunks[:rows, :].astype(F32)
    for i in range(1, count):
        value += chunks[i * rows : (i + 1) * rows, :].astype(F32)
    total[...] = value
    rows = keep.shape[0]
    keep[...] = total[pl.ds(pl.multiple_of(scalars[0] * rows, 8), rows), :]
    send[...] = total[pl.ds(pl.multiple_of((1 - scalars[0]) * rows, 8), rows), :]


def start_loads(scalars, at_order, size, pieces, ready, lanes, sems, first):
    copies = []
    for piece in pieces:
        for row in range(0, piece.shape[0], size):
            i = len(copies)
            at = pl.multiple_of(scalars[at_order + i] * size, size)
            target = ready.at[pl.ds(at, size), lanes]
            copies.append(
                pltpu.make_async_copy(piece.at[pl.ds(row, size), :], target, sems.at[first + i])
            )
    for copy in copies:
        copy.start()
    return copies


def subtract_updates(scalars, plan, update, ready, lanes):
    unit, places, block, at_table = plan[:4]
    for i, (index, row) in enumerate(places):
        at = pl.ds(pl.multiple_of(scalars[at_table + index] * block + row, unit), unit)
        value = update[i * unit : (i + 1) * unit, :].astype(F32)
        ready[at, lanes] = (ready[at, lanes].astype(F32) - value).astype(BF16)


def whole_kernel(plan, scalars, mine, other, inverse, panel, *refs):
    at_order, size, n_pieces, n_next = plan[4:]
    pieces, refs = refs[: 2 * n_pieces], refs[2 * n_pieces :]
    nexts, (solved, keep, send) = refs[:n_next], refs[n_next : n_next + 3]
    ready, x_ref, load_sems, sem, sems = refs[-5:]
    core, half = scalars[0], keep.shape[1]
    lanes = [pl.ds(pl.multiple_of(c * half, half), half) for c in (core, 1 - core)]
    runs = load_sems.shape[0] // 2
    arriving = []
    for i in range(2):
        part = pieces[i * n_pieces : (i + 1) * n_pieces]
        arriving += start_loads(
            scalars, at_order + i * runs, size, part, ready, lanes[i], load_sems, i * runs
        )
    for copy in arriving:
        copy.wait()
    copies = start_all(nexts, refs[n_next + 3 : -5], sems)
    subtract_updates(scalars, plan, mine, ready, lanes[0])
    subtract_updates(scalars, plan, other, ready, lanes[1])

    def step(at):
        x_ref[at, :] = dot(inverse[at, :], ready[...]).astype(BF16)

    tiles(inverse.shape[0], step)
    result = pltpu.make_async_copy(x_ref, solved, sem)
    result.start()
    split_panel(core, panel, x_ref, keep, send)
    for copy in [*copies, result]:
        copy.wait()


def half_kernel(plan, turned, at_place, n_chunks, scalars, mine, inverse_a, inverse_b, panel_a, panel_b, *refs):
    at_order, size, n_pieces, n_next = plan[4:]
    pieces, refs = refs[:n_pieces], refs[n_pieces:]
    nexts, refs = refs[:n_next], refs[n_next:]
    chunks, (x_keep, x_send) = refs[:n_chunks], refs[n_chunks : n_chunks + 2]
    ready, update, load_sems, sems = refs[-4:]
    lanes = pl.ds(0, mine.shape[1])
    arriving = start_loads(scalars, at_order, size, pieces, ready, lanes, load_sems, 0)
    for copy in arriving:
        copy.wait()
    copies = start_all(nexts, refs[n_chunks + 2 : -4], sems)
    subtract_updates(scalars, plan, mine, ready, lanes)

    def step(at):
        x_keep[at, :] = dot(inverse_a[at, :], ready[...]).astype(BF16)
        x_send[at, :] = dot(inverse_b[at, :], ready[...]).astype(BF16)

    tiles(inverse_a.shape[0], step)

    def panel_step(at):
        if turned:
            dims = (((0,), (0,)), ((), ()))
            part = lax.dot_general(panel_a[:, at], x_keep[...], dims, preferred_element_type=F32)
            part += lax.dot_general(panel_b[:, at], x_send[...], dims, preferred_element_type=F32)
        else:
            part = dot(panel_a[at, :], x_keep[...]) + dot(panel_b[at, :], x_send[...])
        update[at, :] = part.astype(update.dtype)

    tiles(update.shape[0], panel_step)
    if n_chunks > 1:
        hand_out(scalars[at_place], update, chunks[0], chunks[1:])
    else:
        chunks[0][...] = update[...].astype(BF16)
    for copy in copies:
        copy.wait()


def in_vmem(arrays):
    return [(aval(*v.shape, BF16), True) for v in arrays]


def solve_whole(scalars, plan, mine, other, inverse, panel, pieces, nexts):
    (rows, depth), half = inverse.shape, mine.shape[1]
    outs = [(aval(rows, 2 * half, BF16), False)]
    outs += [(aval(panel.shape[0], half, t), True) for t in (F32, BF16)]
    return kernel_call(
        functools.partial(whole_kernel, plan),
        outs + in_vmem(nexts),
        scalars,
        [mine, other, inverse, panel],
        [*pieces, *nexts],
        [
            pltpu.VMEM((depth, 2 * half), BF16),
            pltpu.VMEM((rows, 2 * half), BF16),
            pltpu.SemaphoreType.DMA((2 * depth // plan[5],)),
            pltpu.SemaphoreType.DMA,
            pltpu.SemaphoreType.DMA((max(1, len(nexts)),)),
        ],
        limit=14,
    )


def solve_half(scalars, plan, mine, inverses, panels, pieces, nexts, update_rows, at_place, masks):
    (rows, depth), half = inverses[0].shape, mine.shape[1]
    chunks = chunks_of(update_rows, half, masks) if masks else [(aval(update_rows, half, BF16), True)]
    outs = chunks + [(aval(rows, half, BF16), True)] * 2
    turned = panels[0].shape[0] != update_rows
    return kernel_call(
        functools.partial(half_kernel, plan, turned, at_place, len(chunks)),
        outs + in_vmem(nexts),
        scalars,
        [mine, *inverses, *panels],
        [*pieces, *nexts],
        [
            pltpu.VMEM((depth, half), BF16),
            pltpu.VMEM((update_rows, half), F32),
            pltpu.SemaphoreType.DMA((depth // plan[5],)),
            pltpu.SemaphoreType.DMA((max(1, len(nexts)),)),
        ],
        limit=12,
    )


def per_device(
    loads_first,
    loads_second,
    loads_third,
    loads_fourth,
    inverse_first,
    inverse_second,
    inverse_third,
    inverse_fourth,
    panel_first,
    panel_second,
    panel_third,
    panel_fourth,
    blocks_first,
    blocks_second,
    blocks_third,
):
    n_y, n_rows = lax.axis_size("y"), 2 * lax.axis_size("y")
    core, x_index, y_index = (lax.axis_index(a) for a in ("core", "x", "y"))
    z1, z2 = lax.axis_index("z1"), lax.axis_index("z2")
    row_index = y_index * 2 + core
    z_index = z2 * 2 + z1
    leaf = (lax.axis_index("hi") * 4 + z_index) * 2 + x_index
    mask_x, mask_z1, mask_z2 = n_rows, 2 * n_rows, 4 * n_rows
    y_masks = [2 * y for y in range(1, n_y)]
    plane_masks = [(x, y) for y in range(n_y) for x in range(2)]
    update_rows, width = panel_first.shape[0], blocks_first.shape[1]
    block = update_rows // width
    rows, depth = inverse_first.shape[0], loads_first.shape[0]
    cols = loads_first.shape[1]
    half = cols // 2

    values = [core, row_index, row_index ^ 1]
    for mask in y_masks:
        values += [row_index ^ mask, row_index ^ mask ^ 1]
    at_place = len(values)
    values += [y_index, x_index * n_y + y_index]
    column = [0, *y_masks]
    plane = [x * mask_x + y * 2 for x in range(2) for y in range(n_y)]
    at_order = []
    for planes in ([0], [z1, z1 ^ 1], [z_index, z_index ^ 2, z_index ^ 1, z_index ^ 3]):
        at_order.append(len(values))
        for x, y in plane_masks:
            place = ((x_index ^ x) * n_y + (y_index ^ y)) * 2
            for z in planes:
                values += [z * 2 * n_rows + place + (core ^ other) for other in range(2)]
        if len(planes) == 1:
            for x, y in plane_masks:
                place = ((x_index ^ x) * n_y + (y_index ^ y)) * 2
                values += [place + (core ^ other) for other in (1, 0)]
    at_table = [len(values) + 2 * width * i for i in range(3)]
    children = [(leaf >> 1) * 2, (leaf >> 1) * 2 + 1]
    parts = [jnp.stack([jnp.asarray(v, jnp.int32) for v in values])]
    for table, pair in (
        (blocks_first, children),
        (blocks_second, [leaf >> 1, (leaf >> 1) ^ 1]),
        (blocks_third, [leaf >> 2, (leaf >> 2) ^ 1]),
    ):
        parts += [lax.dynamic_index_in_dim(table, c, 0, keepdims=False) for c in pair]
    scalars = jnp.concatenate(parts)
    scalars, loads_second, loads_third, loads_fourth = lax.optimization_barrier(
        (scalars, loads_second, loads_third, loads_fourth)
    )

    tie = lax.optimization_barrier

    n_far = 2 * len(y_masks)
    sibling = permute(loads_first, 1)
    shards = [permute(loads_first, mask, upward=True) for mask in y_masks]
    loads = [loads_second, loads_third, loads_fourth]
    sizes = [v.shape[0] for v in loads]
    keep, send = kernel_call(
        split_kernel,
        [(aval(sum(sizes), half, BF16), True)] * 2,
        scalars,
        [],
        loads,
        [pltpu.VMEM((sum(sizes), cols), BF16), pltpu.SemaphoreType.DMA((len(loads),))],
    )
    received = permute(send, 1)
    keep, received, sibling, inverse_third, panel_third = tie(
        (keep, received, sibling, inverse_third, panel_third)
    )
    inverses = inverse_third, permute(inverse_third, 1)
    panels = panel_third, permute(panel_third, 1)
    acc, far, panel = kernel_call(
        near_kernel,
        [
            (aval(rows, cols, F32), True),
            (aval(rows, n_far * depth, BF16), True),
            (aval(*panel_first.shape, BF16), True),
        ],
        scalars,
        [loads_first, sibling],
        [inverse_first, panel_first],
        [
            pltpu.VMEM((rows, 2 * depth), BF16),
            pltpu.SemaphoreType.DMA((2 * (rows // row_tile(rows)) + n_far + 1,)),
        ],
        limit=16,
    )
    runs = [(sum(sizes[:i]), n) for i, n in enumerate(sizes)]
    groups = [[run] for run in runs]
    own_second, half_third, half_fourth = kernel_call(
        functools.partial(pack_kernel, groups),
        [(aval(2 * sum(n for _, n in group), half, BF16), True) for group in groups],
        scalars,
        [keep, received],
    )
    x_second = permute(own_second, mask_x)
    by_z2 = permute(half_fourth, mask_z2)
    acc, by_z2 = tie((acc, by_z2))
    half_later = jnp.concatenate([half_third, half_fourth, by_z2], 0)
    by_z1 = permute(half_later, mask_z1)
    shards, acc, far, panel, own_second, x_second, inverses, panels = tie(
        (shards, acc, far, panel, own_second, x_second, inverses, panels)
    )

    pieces = [v for shard in shards for v in (shard, permute(shard, 1))]
    y_second = [permute(own_second, mask) for mask in y_masks]
    nexts = [inverse_second, panel_second]
    solved_first, keep, send, inverse_second, panel_second = kernel_call(
        functools.partial(far_kernel, n_far, len(nexts)),
        [
            (aval(rows, cols, BF16), False),
            (aval(update_rows, half, F32), True),
            (aval(update_rows, half, BF16), True),
        ]
        + in_vmem(nexts),
        scalars,
        [acc, panel, far, *pieces],
        nexts,
        [
            pltpu.VMEM((rows, cols), BF16),
            pltpu.SemaphoreType.DMA,
            pltpu.SemaphoreType.DMA((len(nexts),)),
        ],
    )
    keep, send, y_second, by_z1 = tie((keep, send, y_second, by_z1))
    chunks = pair_sum(keep, send, scalars, at_place, column)

    def with_x(x_piece, own, y_pieces):
        pieces = [own, x_piece]
        for piece in y_pieces:
            pieces += [piece, permute(piece, mask_x)]
        return pieces

    pieces_second = with_x(x_second, own_second, y_second)
    early = [own_second, x_second, *y_second]
    across_early = [permute(piece, 1) for piece in early]
    cut = 2 * sizes[1]
    own_third = jnp.concatenate([half_later[:cut], by_z1[:cut]], 0)
    own_fourth = jnp.concatenate([half_later[cut:], by_z1[cut:]], 0)
    part = reduce_chunks(chunks, column, scalars)
    part, pieces_second, across_early, own_third, own_fourth = tie(
        (part, pieces_second, across_early, own_third, own_fourth)
    )

    def spread(value):
        return lax.all_gather(value, PLANE, axis=0, tiled=True)

    def plan_of(level, chunk, both):
        unit = math.gcd(chunk, block)
        places = []
        for place in range(2 * n_y):
            for child in range(2) if both else [place // n_y]:
                start = (place if both else place % n_y) * chunk
                for row in range(start, start + chunk, unit):
                    places.append((child * width + row // block, row % block))
        n_next = 4 if level < 2 else 0
        return unit, places, block, at_table[level], at_order[level], sizes[level], n_pieces, n_next

    n_pieces = len(plane_masks)

    across = across_early[:2]
    for i in range(len(y_masks)):
        across += [across_early[2 + i], permute(pieces_second[3 + 2 * i], 1)]
    pieces_second += across
    mine = spread(part)
    other = permute(mine, 1)
    mine, other, pieces_second, own_third, own_fourth = tie(
        (mine, other, pieces_second, own_third, own_fourth)
    )
    x_third = permute(own_third, mask_x)
    y_third = [permute(own_third, mask) for mask in y_masks]
    solved_second, keep, send, *nexts = solve_whole(
        scalars,
        plan_of(0, part.shape[0], False),
        mine,
        other,
        inverse_second,
        panel_second,
        pieces_second,
        [*inverses, *panels],
    )
    keep, send, x_third, y_third = tie((keep, send, x_third, y_third))

    chunks = pair_sum(keep, send, scalars, at_place + 1, plane)
    chunks, y_third, inverse_fourth, panel_fourth = tie(
        (chunks, y_third, inverse_fourth, panel_fourth)
    )
    part = reduce_chunks(chunks, plane, scalars)
    part, y_third = tie((part, y_third))
    sibling = permute(part, mask_z1)
    pieces_third = with_x(x_third, own_third, y_third)
    panel_fourth = panel_fourth.T
    fourth = [
        inverse_fourth, permute(inverse_fourth, 1), panel_fourth, permute(panel_fourth, 1),
    ]
    part, sibling, pieces_third, fourth = tie((part, sibling, pieces_third, fourth))
    mine = spread(jnp.concatenate([part, sibling], 0))
    mine, own_fourth = tie((mine, own_fourth))
    x_fourth = permute(own_fourth, mask_x)
    y_fourth = [permute(own_fourth, mask) for mask in y_masks]
    *chunks, keep, send, a, b, c, d = solve_half(
        scalars,
        plan_of(1, part.shape[0], True),
        mine,
        nexts[:2],
        nexts[2:],
        pieces_third,
        fourth,
        update_rows,
        at_place + 1,
        plane,
    )
    fourth = [a, b, c, d]
    chunks, keep, send, x_fourth, y_fourth = tie((chunks, keep, send, x_fourth, y_fourth))

    part = reduce_chunks(chunks, plane, scalars)
    part, keep, send, x_fourth, y_fourth = tie((part, keep, send, x_fourth, y_fourth))
    pieces_fourth = with_x(x_fourth, own_fourth, y_fourth)
    solved_third = join_columns(scalars, keep, permute(send, 1))
    part = (part.astype(F32) + permute(part, mask_z1).astype(F32)).astype(BF16)
    sibling = permute(part, mask_z2)
    part, sibling, pieces_fourth, solved_third = tie((part, sibling, pieces_fourth, solved_third))
    mine = spread(jnp.concatenate([part, sibling], 0))
    update, keep_fourth, send_fourth = solve_half(
        scalars,
        plan_of(2, part.shape[0], True),
        mine,
        fourth[:2],
        fourth[2:],
        pieces_fourth,
        [],
        update_rows,
        0,
        [],
    )
    solved_fourth = join_columns(scalars, keep_fourth, permute(send_fourth, 1))
    everywhere = ("z2", "z1", "x", "y")
    count = lax.axis_size(everywhere)
    arrived = lax.all_to_all(update, everywhere, 0, 0, tiled=True)
    chunk = update_rows // count
    keep, send = kernel_call(
        functools.partial(core_split_kernel, count),
        [(aval(chunk // 2, half, F32), True)] * 2,
        scalars,
        [arrived],
        scratch=[pltpu.VMEM((chunk, half), F32)],
    )
    ancestor = join_columns(scalars, keep, permute(send, 1))
    return solved_first, solved_second, solved_third, solved_fourth, ancestor


def solution(mesh):
    n_leaf, n_rows = mesh.shape["leaf"], mesh.shape["rows"]
    fine = Mesh(mesh.devices.reshape(n_leaf // 8, 2, 2, 2, n_rows // 2, 2), AXES)
    rows, cols = P(AXES, None), P(None, AXES)
    return jax.shard_map(
        per_device,
        mesh=fine,
        in_specs=(rows,) * 8 + (cols,) * 4 + (P(),) * 3,
        out_specs=(rows,) * 5,
        check_vma=False,
    )
```

```python
import functools
import math

import jax
import jax.numpy as jnp
from jax import lax
from jax.experimental import pallas as pl
from jax.experimental.pallas import tpu as pltpu
from jax.sharding import Mesh
from jax.sharding import PartitionSpec as P

BF16 = jnp.bfloat16
F32 = jnp.float32
AXES = ("hi", "z2", "z1", "x", "y", "core")
PLANE = ("x", "y")
VMEM = pl.BlockSpec(memory_space=pltpu.VMEM)
SMEM = pl.BlockSpec(memory_space=pltpu.SMEM)
ANY = pl.BlockSpec(memory_space=pl.ANY)
MIB = 1 << 20


def permute(value, mask, upward=False):
    total = lax.axis_size(AXES)
    pairs = [(i, i ^ mask) for i in range(total) if not upward or (i ^ mask) > i]
    return lax.ppermute(value, AXES, pairs)


def row_tile(rows):
    return next(t for t in (512, 384, 256, 192, 128, 96, 64, 48, 32, 16) if rows % t == 0)


def aval(rows, cols, dtype):
    return jax.ShapeDtypeStruct((rows, cols), dtype)


def kernel_call(kernel, outs, scalars, vmem, hbm=(), scratch=(), limit=8):
    operands = [pltpu.with_memory_space_constraint(o, pltpu.VMEM) for o in vmem]
    return pl.pallas_call(
        kernel,
        out_shape=[pltpu.VMEM(o.shape, o.dtype) if inside else o for o, inside in outs],
        in_specs=[SMEM] + [VMEM] * len(vmem) + [ANY] * len(hbm),
        out_specs=[ANY if inside is False else VMEM for _, inside in outs],
        scratch_shapes=list(scratch),
        compiler_params=pltpu.CompilerParams(vmem_limit_bytes=limit * MIB),
        cost_estimate=pl.CostEstimate(flops=1, bytes_accessed=1, transcendentals=0),
    )(scalars, *operands, *[pltpu.with_memory_space_constraint(o, pltpu.HBM) for o in hbm])


def tiles(rows, step):
    tile = row_tile(rows)

    def body(i, carry):
        step(pl.ds(pl.multiple_of(i * tile, tile), tile))
        return carry

    lax.fori_loop(0, rows // tile, body, 0)


def dot(a, b):
    return jnp.dot(a, b, preferred_element_type=F32)


def start_all(sources, targets, sems):
    copies = [
        pltpu.make_async_copy(source, target, sems.at[i])
        for i, (source, target) in enumerate(zip(sources, targets))
    ]
    for copy in copies:
        copy.start()
    return copies


def near_kernel(scalars, b0, b1, inverse, panel, acc, far, panel_out, near, sems):
    rows, depth = inverse.shape[0], b0.shape[0]
    tile = row_tile(rows)
    n_far = far.shape[1] // depth
    columns = [
        pl.ds(pl.multiple_of(scalars[1 + i] * depth, depth), depth) for i in range(2 + n_far)
    ]
    sources, targets = [], []
    for i in range(rows // tile):
        at = pl.ds(i * tile, tile)
        for j in range(2):
            sources.append(inverse.at[at, columns[j]])
            targets.append(near.at[at, pl.ds(j * depth, depth)])
    for j in range(n_far):
        sources.append(inverse.at[:, columns[2 + j]])
        targets.append(far.at[:, pl.ds(j * depth, depth)])
    sources.append(panel)
    targets.append(panel_out)
    copies = start_all(sources, targets, sems)
    for i in range(rows // tile):
        at = pl.ds(i * tile, tile)
        copies[2 * i].wait()
        copies[2 * i + 1].wait()
        acc[at, :] = dot(near[at, :depth], b0[...]) + dot(near[at, depth:], b1[...])
    for copy in copies[2 * (rows // tile) :]:
        copy.wait()


def split_panel(core, panel, x_ref, keep, send):
    half = keep.shape[1]

    def step(at):
        part = dot(panel[at, :], x_ref[...])
        low, high = part[:, :half], part[:, half:]
        keep[at, :] = jnp.where(core == 0, low, high)
        send[at, :] = jnp.where(core == 0, high, low).astype(BF16)

    tiles(panel.shape[0], step)


def far_kernel(n_far, n_next, scalars, acc, panel, far, *refs):
    pieces, refs = refs[:n_far], refs[n_far:]
    solved, keep, send = refs[n_next : n_next + 3]
    x_ref, sem, sems = refs[-3:]
    copies = start_all(refs[:n_next], refs[n_next + 3 : -3], sems)
    depth = pieces[0].shape[0]

    def step(at):
        total = acc[at, :]
        for j, piece in enumerate(pieces):
            total += dot(far[at, j * depth : (j + 1) * depth], piece[...])
        x_ref[at, :] = total.astype(BF16)

    tiles(far.shape[0], step)
    result = pltpu.make_async_copy(x_ref, solved, sem)
    result.start()
    split_panel(scalars[0], panel, x_ref, keep, send)
    for copy in [*copies, result]:
        copy.wait()


def split_kernel(scalars, *refs):
    *arrays, keep, send, held, sems = refs
    core, half, first, targets = scalars[0], keep.shape[1], 0, []
    for array in arrays:
        targets.append(held.at[pl.ds(first, array.shape[0]), :])
        first += array.shape[0]
    for copy in start_all(arrays, targets, sems):
        copy.wait()
    low, high = held[:, :half], held[:, half:]
    keep[...] = jnp.where(core == 0, low, high)
    send[...] = jnp.where(core == 0, high, low)


def pack_kernel(groups, scalars, keep, received, *outs):
    core = scalars[0]
    for group, out in zip(groups, outs):
        at = 0
        for first, rows in group:
            for lane, part in ((core, keep), (1 - core, received)):
                target = pl.ds(pl.multiple_of(at + lane * rows, math.gcd(rows, 16)), rows)
                out[target, :] = part[first : first + rows, :]
            at += 2 * rows


def join_kernel(scalars, own, other, out):
    half = own.shape[1]
    out[:, :half] = jnp.where(scalars[0] == 0, own[...], other[...])
    out[:, half:] = jnp.where(scalars[0] == 0, other[...], own[...])


def join_all_kernel(scalars, *refs):
    count = len(refs) // 3
    for i in range(count):
        join_kernel(scalars, refs[2 * i], refs[2 * i + 1], refs[2 * count + i])


def join_columns(scalars, pairs):
    return kernel_call(
        join_all_kernel,
        [(aval(own.shape[0], 2 * own.shape[1], own.dtype), None) for own, _ in pairs],
        scalars,
        [v for pair in pairs for v in pair],
    )


def hand_out(place, value, own, sends):
    rows = own.shape[0]
    for mask, out in enumerate([own, *sends]):
        at = pl.ds(pl.multiple_of((place ^ mask) * rows, rows), rows)
        out[...] = value[at, :].astype(out.dtype)


def pair_sum_kernel(at_place, scalars, keep, received, own, *rest):
    *sends, total = rest
    total[...] = keep[...] + received[...].astype(F32)
    hand_out(scalars[at_place], total, own, sends)


def sum_kernel(scalars, own, *rest):
    total = own[...]
    for other in rest[:-1]:
        total += other[...].astype(F32)
    rest[-1][...] = total.astype(rest[-1].dtype)


def chunks_of(rows, cols, masks):
    rows //= len(masks)
    return [(aval(rows, cols, F32), True)] + [(aval(rows, cols, BF16), True)] * (len(masks) - 1)


def pair_sum(keep, send, scalars, at_place, masks):
    received = permute(send, 1)
    return kernel_call(
        functools.partial(pair_sum_kernel, at_place),
        chunks_of(*keep.shape, masks),
        scalars,
        [keep, received],
        scratch=[pltpu.VMEM(keep.shape, F32)],
    )


def reduce_chunks(chunks, masks, scalars):
    own, *sends = chunks
    arrived = [permute(value, mask) for value, mask in zip(sends, masks[1:])]
    return kernel_call(
        sum_kernel, [(aval(*own.shape, BF16), True)], scalars, [own, *arrived]
    )[0]


def core_split_kernel(count, scalars, chunks, keep, send, total):
    rows = total.shape[0]
    value = chunks[:rows, :].astype(F32)
    for i in range(1, count):
        value += chunks[i * rows : (i + 1) * rows, :].astype(F32)
    total[...] = value
    rows = keep.shape[0]
    keep[...] = total[pl.ds(pl.multiple_of(scalars[0] * rows, 8), rows), :]
    send[...] = total[pl.ds(pl.multiple_of((1 - scalars[0]) * rows, 8), rows), :]


def start_loads(scalars, at_order, size, pieces, ready, lanes, sems, first):
    copies = []
    for piece in pieces:
        for row in range(0, piece.shape[0], size):
            i = len(copies)
            at = pl.multiple_of(scalars[at_order + i] * size, size)
            target = ready.at[pl.ds(at, size), lanes]
            copies.append(
                pltpu.make_async_copy(piece.at[pl.ds(row, size), :], target, sems.at[first + i])
            )
    for copy in copies:
        copy.start()
    return copies


def subtract_updates(scalars, plan, update, ready, lanes):
    unit, places, block, at_table = plan[:4]
    for i, (index, row) in enumerate(places):
        at = pl.ds(pl.multiple_of(scalars[at_table + index] * block + row, unit), unit)
        value = update[i * unit : (i + 1) * unit, :].astype(F32)
        ready[at, lanes] = (ready[at, lanes].astype(F32) - value).astype(BF16)


def whole_kernel(plan, scalars, mine, other, inverse, panel, *refs):
    at_order, size, n_pieces, n_next = plan[4:]
    pieces, refs = refs[: 2 * n_pieces], refs[2 * n_pieces :]
    nexts, (solved, keep, send) = refs[:n_next], refs[n_next : n_next + 3]
    ready, x_ref, load_sems, sem, sems = refs[-5:]
    core, half = scalars[0], keep.shape[1]
    lanes = [pl.ds(pl.multiple_of(c * half, half), half) for c in (core, 1 - core)]
    runs = load_sems.shape[0] // 2
    arriving = []
    for i in range(2):
        part = pieces[i * n_pieces : (i + 1) * n_pieces]
        arriving += start_loads(
            scalars, at_order + i * runs, size, part, ready, lanes[i], load_sems, i * runs
        )
    for copy in arriving:
        copy.wait()
    copies = start_all(nexts, refs[n_next + 3 : -5], sems)
    subtract_updates(scalars, plan, mine, ready, lanes[0])
    subtract_updates(scalars, plan, other, ready, lanes[1])

    def step(at):
        x_ref[at, :] = dot(inverse[at, :], ready[...]).astype(BF16)

    tiles(inverse.shape[0], step)
    result = pltpu.make_async_copy(x_ref, solved, sem)
    result.start()
    split_panel(core, panel, x_ref, keep, send)
    for copy in [*copies, result]:
        copy.wait()


def half_kernel(plan, turned, at_place, n_chunks, scalars, mine, inverse_a, inverse_b, panel_a, panel_b, *refs):
    at_order, size, n_pieces, n_next = plan[4:]
    pieces, refs = refs[:n_pieces], refs[n_pieces:]
    nexts, refs = refs[:n_next], refs[n_next:]
    chunks, (x_keep, x_send) = refs[:n_chunks], refs[n_chunks : n_chunks + 2]
    ready, update, load_sems, sems = refs[-4:]
    lanes = pl.ds(0, mine.shape[1])
    arriving = start_loads(scalars, at_order, size, pieces, ready, lanes, load_sems, 0)
    for copy in arriving:
        copy.wait()
    copies = start_all(nexts, refs[n_chunks + 2 : -4], sems)
    subtract_updates(scalars, plan, mine, ready, lanes)

    def step(at):
        x_keep[at, :] = dot(inverse_a[at, :], ready[...]).astype(BF16)
        x_send[at, :] = dot(inverse_b[at, :], ready[...]).astype(BF16)

    tiles(inverse_a.shape[0], step)

    def panel_step(at):
        if turned:
            dims = (((0,), (0,)), ((), ()))
            part = lax.dot_general(panel_a[:, at], x_keep[...], dims, preferred_element_type=F32)
            part += lax.dot_general(panel_b[:, at], x_send[...], dims, preferred_element_type=F32)
        else:
            part = dot(panel_a[at, :], x_keep[...]) + dot(panel_b[at, :], x_send[...])
        update[at, :] = part.astype(update.dtype)

    tiles(update.shape[0], panel_step)
    if n_chunks > 1:
        hand_out(scalars[at_place], update, chunks[0], chunks[1:])
    else:
        chunks[0][...] = update[...].astype(BF16)
    for copy in copies:
        copy.wait()


def in_vmem(arrays):
    return [(aval(*v.shape, BF16), True) for v in arrays]


def solve_whole(scalars, plan, mine, other, inverse, panel, pieces, nexts):
    (rows, depth), half = inverse.shape, mine.shape[1]
    outs = [(aval(rows, 2 * half, BF16), False)]
    outs += [(aval(panel.shape[0], half, t), True) for t in (F32, BF16)]
    return kernel_call(
        functools.partial(whole_kernel, plan),
        outs + in_vmem(nexts),
        scalars,
        [mine, other, inverse, panel],
        [*pieces, *nexts],
        [
            pltpu.VMEM((depth, 2 * half), BF16),
            pltpu.VMEM((rows, 2 * half), BF16),
            pltpu.SemaphoreType.DMA((2 * depth // plan[5],)),
            pltpu.SemaphoreType.DMA,
            pltpu.SemaphoreType.DMA((max(1, len(nexts)),)),
        ],
        limit=14,
    )


def solve_half(scalars, plan, mine, inverses, panels, pieces, nexts, update_rows, at_place, masks):
    (rows, depth), half = inverses[0].shape, mine.shape[1]
    chunks = chunks_of(update_rows, half, masks) if masks else [(aval(update_rows, half, BF16), True)]
    outs = chunks + [(aval(rows, half, BF16), True)] * 2
    turned = panels[0].shape[0] != update_rows
    return kernel_call(
        functools.partial(half_kernel, plan, turned, at_place, len(chunks)),
        outs + in_vmem(nexts),
        scalars,
        [mine, *inverses, *panels],
        [*pieces, *nexts],
        [
            pltpu.VMEM((depth, half), BF16),
            pltpu.VMEM((update_rows, half), F32),
            pltpu.SemaphoreType.DMA((depth // plan[5],)),
            pltpu.SemaphoreType.DMA((max(1, len(nexts)),)),
        ],
        limit=12,
    )


def per_device(
    loads_first,
    loads_second,
    loads_third,
    loads_fourth,
    inverse_first,
    inverse_second,
    inverse_third,
    inverse_fourth,
    panel_first,
    panel_second,
    panel_third,
    panel_fourth,
    blocks_first,
    blocks_second,
    blocks_third,
):
    n_y, n_rows = lax.axis_size("y"), 2 * lax.axis_size("y")
    core, x_index, y_index = (lax.axis_index(a) for a in ("core", "x", "y"))
    z1, z2 = lax.axis_index("z1"), lax.axis_index("z2")
    row_index = y_index * 2 + core
    z_index = z2 * 2 + z1
    leaf = (lax.axis_index("hi") * 4 + z_index) * 2 + x_index
    mask_x, mask_z1, mask_z2 = n_rows, 2 * n_rows, 4 * n_rows
    y_masks = [2 * y for y in range(1, n_y)]
    plane_masks = [(x, y) for y in range(n_y) for x in range(2)]
    update_rows, width = panel_first.shape[0], blocks_first.shape[1]
    block = update_rows // width
    rows, depth = inverse_first.shape[0], loads_first.shape[0]
    cols = loads_first.shape[1]
    half = cols // 2

    values = [core, row_index, row_index ^ 1]
    for mask in y_masks:
        values += [row_index ^ mask, row_index ^ mask ^ 1]
    at_place = len(values)
    values += [y_index, x_index * n_y + y_index]
    column = [0, *y_masks]
    plane = [x * mask_x + y * 2 for x in range(2) for y in range(n_y)]
    at_order = []
    for planes in ([0], [z1, z1 ^ 1], [z_index, z_index ^ 2, z_index ^ 1, z_index ^ 3]):
        at_order.append(len(values))
        for _ in range(2 if len(planes) == 1 else 1):
            for x, y in plane_masks:
                place = (x_index ^ x) * n_y + (y_index ^ y)
                values += [z * n_rows + place for z in planes]
    at_table = [len(values) + 2 * width * i for i in range(3)]
    children = [(leaf >> 1) * 2, (leaf >> 1) * 2 + 1]
    parts = [jnp.stack([jnp.asarray(v, jnp.int32) for v in values])]
    for table, pair in (
        (blocks_first, children),
        (blocks_second, [leaf >> 1, (leaf >> 1) ^ 1]),
        (blocks_third, [leaf >> 2, (leaf >> 2) ^ 1]),
    ):
        parts += [lax.dynamic_index_in_dim(table, c, 0, keepdims=False) for c in pair]
    scalars = jnp.concatenate(parts)

    tie = lax.optimization_barrier

    n_far = 2 * len(y_masks)
    sibling = permute(loads_first, 1)
    shards = [permute(loads_first, mask, upward=True) for mask in y_masks]
    loads = [loads_second, loads_third, loads_fourth]
    sizes = [v.shape[0] for v in loads]
    keep, send = kernel_call(
        split_kernel,
        [(aval(sum(sizes), half, BF16), True)] * 2,
        core[None].astype(jnp.int32),
        [],
        loads,
        [pltpu.VMEM((sum(sizes), cols), BF16), pltpu.SemaphoreType.DMA((len(loads),))],
    )
    received = permute(send, 1)
    scalars, keep, received, sibling, inverse_third, panel_third = tie(
        (scalars, keep, received, sibling, inverse_third, panel_third)
    )
    inverses = inverse_third, permute(inverse_third, 1)
    panels = panel_third, permute(panel_third, 1)
    acc, far, panel = kernel_call(
        near_kernel,
        [
            (aval(rows, cols, F32), True),
            (aval(rows, n_far * depth, BF16), True),
            (aval(*panel_first.shape, BF16), True),
        ],
        scalars,
        [loads_first, sibling],
        [inverse_first, panel_first],
        [
            pltpu.VMEM((rows, 2 * depth), BF16),
            pltpu.SemaphoreType.DMA((2 * (rows // row_tile(rows)) + n_far + 1,)),
        ],
        limit=16,
    )
    runs = [(sum(sizes[:i]), n) for i, n in enumerate(sizes)]
    groups = [[run] for run in runs]
    own_second, half_third, half_fourth = kernel_call(
        functools.partial(pack_kernel, groups),
        [(aval(2 * sum(n for _, n in group), half, BF16), True) for group in groups],
        scalars,
        [keep, received],
    )
    x_second = permute(own_second, mask_x)
    by_z2 = permute(half_fourth, mask_z2)
    by_z1 = permute(half_third, mask_z1)
    acc, by_z1, by_z2 = tie((acc, by_z1, by_z2))
    own_third = jnp.concatenate([half_third, by_z1], 0)
    half_fourth = jnp.concatenate([half_fourth, by_z2], 0)
    x_third = permute(own_third, mask_x)
    by_z1 = permute(half_fourth, mask_z1)
    shards, acc, far, panel, own_second, x_second, inverses, panels = tie(
        (shards, acc, far, panel, own_second, x_second, inverses, panels)
    )

    pieces = [v for shard in shards for v in (shard, permute(shard, 1))]
    y_second = [permute(own_second, mask) for mask in y_masks]
    nexts = [inverse_second, panel_second]
    solved_first, keep, send, inverse_second, panel_second = kernel_call(
        functools.partial(far_kernel, n_far, len(nexts)),
        [
            (aval(rows, cols, BF16), False),
            (aval(update_rows, half, F32), True),
            (aval(update_rows, half, BF16), True),
        ]
        + in_vmem(nexts),
        scalars,
        [acc, panel, far, *pieces],
        nexts,
        [
            pltpu.VMEM((rows, cols), BF16),
            pltpu.SemaphoreType.DMA,
            pltpu.SemaphoreType.DMA((len(nexts),)),
        ],
    )
    keep, send, y_second, by_z1, x_third = tie((keep, send, y_second, by_z1, x_third))
    chunks = pair_sum(keep, send, scalars, at_place, column)

    def with_x(x_piece, own, y_pieces):
        pieces = [own, x_piece]
        for piece in y_pieces:
            pieces += [piece, permute(piece, mask_x)]
        return pieces

    pieces_second = with_x(x_second, own_second, y_second)
    early = [own_second, x_second, *y_second]
    across_early = [permute(piece, 1) for piece in early]
    own_fourth = jnp.concatenate([half_fourth, by_z1], 0)
    part = reduce_chunks(chunks, column, scalars)
    part, pieces_second, across_early, own_third, own_fourth = tie(
        (part, pieces_second, across_early, own_third, own_fourth)
    )

    def spread(value):
        return lax.all_gather(value, PLANE, axis=0, tiled=True)

    def plan_of(level, chunk, both):
        unit = math.gcd(chunk, block)
        places = []
        for place in range(2 * n_y):
            for child in range(2) if both else [place // n_y]:
                start = (place if both else place % n_y) * chunk
                for row in range(start, start + chunk, unit):
                    places.append((child * width + row // block, row % block))
        n_next = 4 if level < 2 else 0
        return unit, places, block, at_table[level], at_order[level], 2 * sizes[level], n_pieces, n_next

    n_pieces = len(plane_masks)

    across = across_early[:2]
    for i in range(len(y_masks)):
        across += [across_early[2 + i], permute(pieces_second[3 + 2 * i], 1)]
    pieces_second += across
    mine = spread(part)
    mine, pieces_second, own_third, own_fourth = tie(
        (mine, pieces_second, own_third, own_fourth)
    )
    other = permute(mine, 1)
    x_fourth = permute(own_fourth, mask_x)
    y_third = [permute(own_third, mask) for mask in y_masks]
    solved_second, keep, send, *nexts = solve_whole(
        scalars,
        plan_of(0, part.shape[0], False),
        mine,
        other,
        inverse_second,
        panel_second,
        pieces_second,
        [*inverses, *panels],
    )
    keep, send, x_fourth, y_third = tie((keep, send, x_fourth, y_third))

    chunks = pair_sum(keep, send, scalars, at_place + 1, plane)
    chunks, y_third, inverse_fourth, panel_fourth = tie(
        (chunks, y_third, inverse_fourth, panel_fourth)
    )
    part = reduce_chunks(chunks, plane, scalars)
    part, y_third, own_fourth = tie((part, y_third, own_fourth))
    sibling = permute(part, mask_z1)
    pieces_third = with_x(x_third, own_third, y_third)
    y_fourth = [permute(own_fourth, mask) for mask in y_masks]
    panel_fourth = panel_fourth.T
    fourth = [
        inverse_fourth, permute(inverse_fourth, 1), panel_fourth, permute(panel_fourth, 1),
    ]
    part, sibling, pieces_third, fourth, y_fourth = tie(
        (part, sibling, pieces_third, fourth, y_fourth)
    )
    mine = spread(jnp.concatenate([part, sibling], 0))
    mine, own_fourth = tie((mine, own_fourth))
    *chunks, keep, send, a, b, c, d = solve_half(
        scalars,
        plan_of(1, part.shape[0], True),
        mine,
        nexts[:2],
        nexts[2:],
        pieces_third,
        fourth,
        update_rows,
        at_place + 1,
        plane,
    )
    fourth = [a, b, c, d]
    chunks, keep, send = tie((chunks, keep, send))

    part = reduce_chunks(chunks, plane, scalars)
    part, keep, send, y_fourth = tie((part, keep, send, y_fourth))
    pieces_fourth = with_x(x_fourth, own_fourth, y_fourth)
    halves_third = keep, permute(send, 1)
    part = (part.astype(F32) + permute(part, mask_z1).astype(F32)).astype(BF16)
    sibling = permute(part, mask_z2)
    part, sibling, pieces_fourth, halves_third = tie((part, sibling, pieces_fourth, halves_third))
    mine = spread(jnp.concatenate([part, sibling], 0))
    update, keep_fourth, send_fourth = solve_half(
        scalars,
        plan_of(2, part.shape[0], True),
        mine,
        fourth[:2],
        fourth[2:],
        pieces_fourth,
        [],
        update_rows,
        0,
        [],
    )
    halves_fourth = keep_fourth, permute(send_fourth, 1)
    everywhere = ("z2", "z1", "x", "y")
    count = lax.axis_size(everywhere)
    arrived = lax.all_to_all(update, everywhere, 0, 0, tiled=True)
    chunk = update_rows // count
    keep, send = kernel_call(
        functools.partial(core_split_kernel, count),
        [(aval(chunk // 2, half, F32), True)] * 2,
        scalars,
        [arrived],
        scratch=[pltpu.VMEM((chunk, half), F32)],
    )
    solved_third, solved_fourth = join_columns(scalars, [halves_third, halves_fourth])
    ancestor = join_columns(scalars, [(keep, permute(send, 1))])[0]
    return solved_first, solved_second, solved_third, solved_fourth, ancestor


def solution(mesh):
    n_leaf, n_rows = mesh.shape["leaf"], mesh.shape["rows"]
    fine = Mesh(mesh.devices.reshape(n_leaf // 8, 2, 2, 2, n_rows // 2, 2), AXES)
    rows, cols = P(AXES, None), P(None, AXES)
    return jax.shard_map(
        per_device,
        mesh=fine,
        in_specs=(rows,) * 8 + (cols,) * 4 + (P(),) * 3,
        out_specs=(rows,) * 5,
        check_vma=False,
    )
```

```python
import functools
import math

import jax
import jax.numpy as jnp
from jax import lax
from jax.experimental import pallas as pl
from jax.experimental.pallas import tpu as pltpu
from jax.sharding import Mesh
from jax.sharding import PartitionSpec as P

BF16 = jnp.bfloat16
F32 = jnp.float32
AXES = ("hi", "z2", "z1", "x", "y", "core")
PLANE = ("x", "y")
VMEM = pl.BlockSpec(memory_space=pltpu.VMEM)
SMEM = pl.BlockSpec(memory_space=pltpu.SMEM)
ANY = pl.BlockSpec(memory_space=pl.ANY)
MIB = 1 << 20


def permute(value, mask, upward=False):
    total = lax.axis_size(AXES)
    pairs = [(i, i ^ mask) for i in range(total) if not upward or (i ^ mask) > i]
    return lax.ppermute(value, AXES, pairs)


def row_tile(rows):
    return next(t for t in (512, 384, 256, 192, 128, 96, 64, 48, 32, 16) if rows % t == 0)


def aval(rows, cols, dtype):
    return jax.ShapeDtypeStruct((rows, cols), dtype)


def kernel_call(kernel, outs, scalars, vmem, hbm=(), scratch=(), limit=8):
    operands = [pltpu.with_memory_space_constraint(o, pltpu.VMEM) for o in vmem]
    return pl.pallas_call(
        kernel,
        out_shape=[pltpu.VMEM(o.shape, o.dtype) if inside else o for o, inside in outs],
        in_specs=[SMEM] + [VMEM] * len(vmem) + [ANY] * len(hbm),
        out_specs=[ANY if inside is False else VMEM for _, inside in outs],
        scratch_shapes=list(scratch),
        compiler_params=pltpu.CompilerParams(vmem_limit_bytes=limit * MIB),
        cost_estimate=pl.CostEstimate(flops=1, bytes_accessed=1, transcendentals=0),
    )(scalars, *operands, *[pltpu.with_memory_space_constraint(o, pltpu.HBM) for o in hbm])


def tiles(rows, step):
    tile = row_tile(rows)

    def body(i, carry):
        step(pl.ds(pl.multiple_of(i * tile, tile), tile))
        return carry

    lax.fori_loop(0, rows // tile, body, 0)


def dot(a, b):
    return jnp.dot(a, b, preferred_element_type=F32)


def start_all(sources, targets, sems):
    copies = [
        pltpu.make_async_copy(source, target, sems.at[i])
        for i, (source, target) in enumerate(zip(sources, targets))
    ]
    for copy in copies:
        copy.start()
    return copies


def near_kernel(scalars, b0, b1, inverse, panel, acc, far, panel_out, near, sems):
    rows, depth = inverse.shape[0], b0.shape[0]
    tile = row_tile(rows)
    n_far = far.shape[1] // depth
    columns = [
        pl.ds(pl.multiple_of(scalars[1 + i] * depth, depth), depth) for i in range(2 + n_far)
    ]
    sources, targets = [], []
    for i in range(rows // tile):
        at = pl.ds(i * tile, tile)
        for j in range(2):
            sources.append(inverse.at[at, columns[j]])
            targets.append(near.at[at, pl.ds(j * depth, depth)])
    for j in range(n_far):
        sources.append(inverse.at[:, columns[2 + j]])
        targets.append(far.at[:, pl.ds(j * depth, depth)])
    sources.append(panel)
    targets.append(panel_out)
    copies = start_all(sources, targets, sems)
    for i in range(rows // tile):
        at = pl.ds(i * tile, tile)
        copies[2 * i].wait()
        copies[2 * i + 1].wait()
        acc[at, :] = dot(near[at, :depth], b0[...]) + dot(near[at, depth:], b1[...])
    for copy in copies[2 * (rows // tile) :]:
        copy.wait()


def split_panel(core, panel, x_ref, keep, send):
    half = keep.shape[1]

    def step(at):
        part = dot(panel[at, :], x_ref[...])
        low, high = part[:, :half], part[:, half:]
        keep[at, :] = jnp.where(core == 0, low, high)
        send[at, :] = jnp.where(core == 0, high, low).astype(BF16)

    tiles(panel.shape[0], step)


def far_kernel(n_far, n_next, scalars, acc, panel, far, *refs):
    pieces, refs = refs[:n_far], refs[n_far:]
    solved, keep, send = refs[n_next : n_next + 3]
    x_ref, sem, sems = refs[-3:]
    copies = start_all(refs[:n_next], refs[n_next + 3 : -3], sems)
    depth = pieces[0].shape[0]

    def step(at):
        total = acc[at, :]
        for j, piece in enumerate(pieces):
            total += dot(far[at, j * depth : (j + 1) * depth], piece[...])
        x_ref[at, :] = total.astype(BF16)

    tiles(far.shape[0], step)
    result = pltpu.make_async_copy(x_ref, solved, sem)
    result.start()
    split_panel(scalars[0], panel, x_ref, keep, send)
    for copy in [*copies, result]:
        copy.wait()


def split_kernel(scalars, *refs):
    *arrays, keep, send, held, sems = refs
    core, half, first, targets = scalars[0], keep.shape[1], 0, []
    for array in arrays:
        targets.append(held.at[pl.ds(first, array.shape[0]), :])
        first += array.shape[0]
    for copy in start_all(arrays, targets, sems):
        copy.wait()
    low, high = held[:, :half], held[:, half:]
    keep[...] = jnp.where(core == 0, low, high)
    send[...] = jnp.where(core == 0, high, low)


def pack_kernel(groups, scalars, keep, received, *outs):
    core = scalars[0]
    for group, out in zip(groups, outs):
        at = 0
        for first, rows in group:
            for lane, part in ((core, keep), (1 - core, received)):
                target = pl.ds(pl.multiple_of(at + lane * rows, math.gcd(rows, 16)), rows)
                out[target, :] = part[first : first + rows, :]
            at += 2 * rows


def join_kernel(scalars, own, other, out):
    half = own.shape[1]
    out[:, :half] = jnp.where(scalars[0] == 0, own[...], other[...])
    out[:, half:] = jnp.where(scalars[0] == 0, other[...], own[...])


def join_all_kernel(scalars, *refs):
    count = len(refs) // 3
    for i in range(count):
        join_kernel(scalars, refs[2 * i], refs[2 * i + 1], refs[2 * count + i])


def join_columns(scalars, pairs):
    return kernel_call(
        join_all_kernel,
        [(aval(own.shape[0], 2 * own.shape[1], own.dtype), None) for own, _ in pairs],
        scalars,
        [v for pair in pairs for v in pair],
    )


def hand_out(place, value, own, sends):
    rows = own.shape[0]
    for mask, out in enumerate([own, *sends]):
        at = pl.ds(pl.multiple_of((place ^ mask) * rows, rows), rows)
        out[...] = value[at, :].astype(out.dtype)


def pair_sum_kernel(at_place, scalars, keep, received, own, *rest):
    *sends, total = rest
    total[...] = keep[...] + received[...].astype(F32)
    hand_out(scalars[at_place], total, own, sends)


def sum_kernel(scalars, own, *rest):
    total = own[...]
    for other in rest[:-1]:
        total += other[...].astype(F32)
    rest[-1][...] = total.astype(rest[-1].dtype)


def chunks_of(rows, cols, masks):
    rows //= len(masks)
    return [(aval(rows, cols, F32), True)] + [(aval(rows, cols, BF16), True)] * (len(masks) - 1)


def pair_sum(keep, send, scalars, at_place, masks):
    received = permute(send, 1)
    return kernel_call(
        functools.partial(pair_sum_kernel, at_place),
        chunks_of(*keep.shape, masks),
        scalars,
        [keep, received],
        scratch=[pltpu.VMEM(keep.shape, F32)],
    )


def reduce_chunks(chunks, masks, scalars):
    own, *sends = chunks
    arrived = [permute(value, mask) for value, mask in zip(sends, masks[1:])]
    return kernel_call(
        sum_kernel, [(aval(*own.shape, BF16), True)], scalars, [own, *arrived]
    )[0]


def core_split_kernel(count, scalars, chunks, keep, send, total):
    rows = total.shape[0]
    value = chunks[:rows, :].astype(F32)
    for i in range(1, count):
        value += chunks[i * rows : (i + 1) * rows, :].astype(F32)
    total[...] = value
    rows = keep.shape[0]
    keep[...] = total[pl.ds(pl.multiple_of(scalars[0] * rows, 8), rows), :]
    send[...] = total[pl.ds(pl.multiple_of((1 - scalars[0]) * rows, 8), rows), :]


def start_loads(scalars, at_order, size, pieces, ready, lanes, sems, first):
    copies = []
    for piece in pieces:
        for row in range(0, piece.shape[0], size):
            i = len(copies)
            at = pl.multiple_of(scalars[at_order + i] * size, size)
            target = ready.at[pl.ds(at, size), lanes]
            copies.append(
                pltpu.make_async_copy(piece.at[pl.ds(row, size), :], target, sems.at[first + i])
            )
    for copy in copies:
        copy.start()
    return copies


def subtract_updates(scalars, plan, update, ready, lanes):
    unit, places, block, at_table = plan[:4]
    for i, (index, row) in enumerate(places):
        at = pl.ds(pl.multiple_of(scalars[at_table + index] * block + row, unit), unit)
        value = update[i * unit : (i + 1) * unit, :].astype(F32)
        ready[at, lanes] = (ready[at, lanes].astype(F32) - value).astype(BF16)


def subtract_parts(scalars, plan, parts, ready, lanes):
    unit, (width, at_place), block, at_table = plan[:4]
    chunk = parts[0].shape[0] // 2
    for mask, part in enumerate(parts):
        first = (scalars[at_place] ^ mask) * chunk
        for child in range(2):
            for start in range(0, chunk, unit):
                row = first + start
                index = scalars[at_table + child * width + lax.div(row, block)]
                at = pl.ds(pl.multiple_of(index * block + lax.rem(row, block), unit), unit)
                value = part[pl.ds(child * chunk + start, unit), :].astype(F32)
                ready[at, lanes] = (ready[at, lanes].astype(F32) - value).astype(BF16)


def whole_kernel(plan, scalars, mine, other, inverse, panel, *refs):
    at_order, size, n_pieces, n_next = plan[4:]
    pieces, refs = refs[: 2 * n_pieces], refs[2 * n_pieces :]
    nexts, (solved, keep, send) = refs[:n_next], refs[n_next : n_next + 3]
    ready, x_ref, load_sems, sem, sems = refs[-5:]
    core, half = scalars[0], keep.shape[1]
    lanes = [pl.ds(pl.multiple_of(c * half, half), half) for c in (core, 1 - core)]
    runs = load_sems.shape[0] // 2
    arriving = []
    for i in range(2):
        part = pieces[i * n_pieces : (i + 1) * n_pieces]
        arriving += start_loads(
            scalars, at_order + i * runs, size, part, ready, lanes[i], load_sems, i * runs
        )
    for copy in arriving:
        copy.wait()
    copies = start_all(nexts, refs[n_next + 3 : -5], sems)
    subtract_updates(scalars, plan, mine, ready, lanes[0])
    subtract_updates(scalars, plan, other, ready, lanes[1])

    def step(at):
        x_ref[at, :] = dot(inverse[at, :], ready[...]).astype(BF16)

    tiles(inverse.shape[0], step)
    result = pltpu.make_async_copy(x_ref, solved, sem)
    result.start()
    split_panel(core, panel, x_ref, keep, send)
    for copy in [*copies, result]:
        copy.wait()


def half_kernel(plan, turned, at_place, n_chunks, n_parts, scalars, *refs):
    parts, refs = refs[:n_parts], refs[n_parts:]
    (inverse_a, inverse_b, panel_a, panel_b), refs = refs[:4], refs[4:]
    at_order, size, n_pieces, n_next = plan[4:]
    pieces, refs = refs[:n_pieces], refs[n_pieces:]
    nexts, refs = refs[:n_next], refs[n_next:]
    chunks, (x_keep, x_send) = refs[:n_chunks], refs[n_chunks : n_chunks + 2]
    ready, update, load_sems, sems = refs[-4:]
    lanes = pl.ds(0, parts[0].shape[1])
    arriving = start_loads(scalars, at_order, size, pieces, ready, lanes, load_sems, 0)
    for copy in arriving:
        copy.wait()
    copies = start_all(nexts, refs[n_chunks + 2 : -4], sems)
    subtract_parts(scalars, plan, parts, ready, lanes)

    def step(at):
        x_keep[at, :] = dot(inverse_a[at, :], ready[...]).astype(BF16)
        x_send[at, :] = dot(inverse_b[at, :], ready[...]).astype(BF16)

    tiles(inverse_a.shape[0], step)

    def panel_step(at):
        if turned:
            dims = (((0,), (0,)), ((), ()))
            part = lax.dot_general(panel_a[:, at], x_keep[...], dims, preferred_element_type=F32)
            part += lax.dot_general(panel_b[:, at], x_send[...], dims, preferred_element_type=F32)
        else:
            part = dot(panel_a[at, :], x_keep[...]) + dot(panel_b[at, :], x_send[...])
        update[at, :] = part.astype(update.dtype)

    tiles(update.shape[0], panel_step)
    if n_chunks > 1:
        hand_out(scalars[at_place], update, chunks[0], chunks[1:])
    else:
        chunks[0][...] = update[...].astype(BF16)
    for copy in copies:
        copy.wait()


def in_vmem(arrays):
    return [(aval(*v.shape, BF16), True) for v in arrays]


def solve_whole(scalars, plan, mine, other, inverse, panel, pieces, nexts):
    (rows, depth), half = inverse.shape, mine.shape[1]
    outs = [(aval(rows, 2 * half, BF16), False)]
    outs += [(aval(panel.shape[0], half, t), True) for t in (F32, BF16)]
    return kernel_call(
        functools.partial(whole_kernel, plan),
        outs + in_vmem(nexts),
        scalars,
        [mine, other, inverse, panel],
        [*pieces, *nexts],
        [
            pltpu.VMEM((depth, 2 * half), BF16),
            pltpu.VMEM((rows, 2 * half), BF16),
            pltpu.SemaphoreType.DMA((2 * depth // plan[5],)),
            pltpu.SemaphoreType.DMA,
            pltpu.SemaphoreType.DMA((max(1, len(nexts)),)),
        ],
        limit=14,
    )


def solve_half(scalars, plan, parts, inverses, panels, pieces, nexts, update_rows, at_place, masks):
    (rows, depth), half = inverses[0].shape, parts[0].shape[1]
    chunks = chunks_of(update_rows, half, masks) if masks else [(aval(update_rows, half, BF16), True)]
    outs = chunks + [(aval(rows, half, BF16), True)] * 2
    turned = panels[0].shape[0] != update_rows
    return kernel_call(
        functools.partial(half_kernel, plan, turned, at_place, len(chunks), len(parts)),
        outs + in_vmem(nexts),
        scalars,
        [*parts, *inverses, *panels],
        [*pieces, *nexts],
        [
            pltpu.VMEM((depth, half), BF16),
            pltpu.VMEM((update_rows, half), F32),
            pltpu.SemaphoreType.DMA((depth // plan[5],)),
            pltpu.SemaphoreType.DMA((max(1, len(nexts)),)),
        ],
        limit=12,
    )


def per_device(
    loads_first,
    loads_second,
    loads_third,
    loads_fourth,
    inverse_first,
    inverse_second,
    inverse_third,
    inverse_fourth,
    panel_first,
    panel_second,
    panel_third,
    panel_fourth,
    blocks_first,
    blocks_second,
    blocks_third,
):
    n_y, n_rows = lax.axis_size("y"), 2 * lax.axis_size("y")
    core, x_index, y_index = (lax.axis_index(a) for a in ("core", "x", "y"))
    z1, z2 = lax.axis_index("z1"), lax.axis_index("z2")
    row_index = y_index * 2 + core
    z_index = z2 * 2 + z1
    leaf = (lax.axis_index("hi") * 4 + z_index) * 2 + x_index
    mask_x, mask_z1, mask_z2 = n_rows, 2 * n_rows, 4 * n_rows
    y_masks = [2 * y for y in range(1, n_y)]
    plane_masks = [(x, y) for y in range(n_y) for x in range(2)]
    update_rows, width = panel_first.shape[0], blocks_first.shape[1]
    block = update_rows // width
    rows, depth = inverse_first.shape[0], loads_first.shape[0]
    cols = loads_first.shape[1]
    half = cols // 2

    values = [core, row_index, row_index ^ 1]
    for mask in y_masks:
        values += [row_index ^ mask, row_index ^ mask ^ 1]
    at_place = len(values)
    values += [y_index, x_index * n_y + y_index]
    column = [0, *y_masks]
    plane = [x * mask_x + y * 2 for x in range(2) for y in range(n_y)]
    at_order = []
    for planes in ([0], [z1, z1 ^ 1], [z_index, z_index ^ 2, z_index ^ 1, z_index ^ 3]):
        at_order.append(len(values))
        for _ in range(2 if len(planes) == 1 else 1):
            for x, y in plane_masks:
                place = (x_index ^ x) * n_y + (y_index ^ y)
                values += [z * n_rows + place for z in planes]
    at_table = [len(values) + 2 * width * i for i in range(3)]
    children = [(leaf >> 1) * 2, (leaf >> 1) * 2 + 1]
    parts = [jnp.stack([jnp.asarray(v, jnp.int32) for v in values])]
    for table, pair in (
        (blocks_first, children),
        (blocks_second, [leaf >> 1, (leaf >> 1) ^ 1]),
        (blocks_third, [leaf >> 2, (leaf >> 2) ^ 1]),
    ):
        parts += [lax.dynamic_index_in_dim(table, c, 0, keepdims=False) for c in pair]
    scalars = jnp.concatenate(parts)

    tie = lax.optimization_barrier

    n_far = 2 * len(y_masks)
    sibling = permute(loads_first, 1)
    shards = [permute(loads_first, mask, upward=True) for mask in y_masks]
    loads = [loads_second, loads_third, loads_fourth]
    sizes = [v.shape[0] for v in loads]
    keep, send = kernel_call(
        split_kernel,
        [(aval(sum(sizes), half, BF16), True)] * 2,
        core[None].astype(jnp.int32),
        [],
        loads,
        [pltpu.VMEM((sum(sizes), cols), BF16), pltpu.SemaphoreType.DMA((len(loads),))],
    )
    received = permute(send, 1)
    scalars, keep, received, sibling, inverse_third = tie(
        (scalars, keep, received, sibling, inverse_third)
    )
    inverses = inverse_third, permute(inverse_third, 1)
    acc, far, panel = kernel_call(
        near_kernel,
        [
            (aval(rows, cols, F32), True),
            (aval(rows, n_far * depth, BF16), True),
            (aval(*panel_first.shape, BF16), True),
        ],
        scalars,
        [loads_first, sibling],
        [inverse_first, panel_first],
        [
            pltpu.VMEM((rows, 2 * depth), BF16),
            pltpu.SemaphoreType.DMA((2 * (rows // row_tile(rows)) + n_far + 1,)),
        ],
        limit=16,
    )
    runs = [(sum(sizes[:i]), n) for i, n in enumerate(sizes)]
    groups = [[run] for run in runs]
    own_second, half_third, half_fourth = kernel_call(
        functools.partial(pack_kernel, groups),
        [(aval(2 * sum(n for _, n in group), half, BF16), True) for group in groups],
        scalars,
        [keep, received],
    )
    x_second = permute(own_second, mask_x)
    by_z2 = permute(half_fourth, mask_z2)
    by_z1 = permute(half_third, mask_z1)
    acc, by_z1, by_z2 = tie((acc, by_z1, by_z2))
    own_third = jnp.concatenate([half_third, by_z1], 0)
    half_fourth = jnp.concatenate([half_fourth, by_z2], 0)
    x_third = permute(own_third, mask_x)
    by_z1 = permute(half_fourth, mask_z1)
    shards, acc, far, panel, own_second, x_second, inverses = tie(
        (shards, acc, far, panel, own_second, x_second, inverses)
    )

    pieces = [v for shard in shards for v in (shard, permute(shard, 1))]
    y_second = [permute(own_second, mask) for mask in y_masks]
    nexts = [inverse_second, panel_second]
    solved_first, keep, send, inverse_second, panel_second = kernel_call(
        functools.partial(far_kernel, n_far, len(nexts)),
        [
            (aval(rows, cols, BF16), False),
            (aval(update_rows, half, F32), True),
            (aval(update_rows, half, BF16), True),
        ]
        + in_vmem(nexts),
        scalars,
        [acc, panel, far, *pieces],
        nexts,
        [
            pltpu.VMEM((rows, cols), BF16),
            pltpu.SemaphoreType.DMA,
            pltpu.SemaphoreType.DMA((len(nexts),)),
        ],
    )
    keep, send, y_second, by_z1, x_third = tie((keep, send, y_second, by_z1, x_third))
    chunks = pair_sum(keep, send, scalars, at_place, column)
    chunks, panel_third = tie((chunks, panel_third))
    panels = panel_third, permute(panel_third, 1)

    def with_x(x_piece, own, y_pieces):
        pieces = [own, x_piece]
        for piece in y_pieces:
            pieces += [piece, permute(piece, mask_x)]
        return pieces

    pieces_second = with_x(x_second, own_second, y_second)
    early = [own_second, x_second, *y_second]
    across_early = [permute(piece, 1) for piece in early]
    own_fourth = jnp.concatenate([half_fourth, by_z1], 0)
    part = reduce_chunks(chunks, column, scalars)
    part, pieces_second, across_early, own_third, own_fourth = tie(
        (part, pieces_second, across_early, own_third, own_fourth)
    )

    def spread(value):
        return lax.all_gather(value, PLANE, axis=0, tiled=True)

    def spread_both(own, sib):
        both = jnp.concatenate([own, sib], 0)
        return [both] + [permute(both, mask) for mask in plane[1:]]

    def plan_of(level, chunk):
        unit = math.gcd(chunk, block)
        places = width, at_place + 1
        if level == 0:
            rows = [divmod(row, block) for row in range(0, update_rows, unit)]
            places = [(child * width + i, row) for child in range(2) for i, row in rows]
        n_next = 4 if level < 2 else 0
        return unit, places, block, at_table[level], at_order[level], 2 * sizes[level], n_pieces, n_next

    n_pieces = len(plane_masks)

    across = across_early[:2]
    for i in range(len(y_masks)):
        across += [across_early[2 + i], permute(pieces_second[3 + 2 * i], 1)]
    pieces_second += across
    mine = spread(part)
    mine, pieces_second, own_third, own_fourth = tie(
        (mine, pieces_second, own_third, own_fourth)
    )
    other = permute(mine, 1)
    x_fourth = permute(own_fourth, mask_x)
    y_third = [permute(own_third, mask) for mask in y_masks]
    solved_second, keep, send, *nexts = solve_whole(
        scalars,
        plan_of(0, part.shape[0]),
        mine,
        other,
        inverse_second,
        panel_second,
        pieces_second,
        [*inverses, *panels],
    )
    keep, send, x_fourth, y_third = tie((keep, send, x_fourth, y_third))

    chunks = pair_sum(keep, send, scalars, at_place + 1, plane)
    chunks, y_third, inverse_fourth, panel_fourth = tie(
        (chunks, y_third, inverse_fourth, panel_fourth)
    )
    part = reduce_chunks(chunks, plane, scalars)
    part, y_third, own_fourth = tie((part, y_third, own_fourth))
    sibling = permute(part, mask_z1)
    pieces_third = with_x(x_third, own_third, y_third)
    y_fourth = [permute(own_fourth, mask) for mask in y_masks]
    panel_fourth = panel_fourth.T
    fourth = [
        inverse_fourth, permute(inverse_fourth, 1), panel_fourth, permute(panel_fourth, 1),
    ]
    part, sibling, pieces_third, fourth, y_fourth = tie(
        (part, sibling, pieces_third, fourth, y_fourth)
    )
    parts = spread_both(part, sibling)
    *chunks, keep, send, a, b, c, d = solve_half(
        scalars,
        plan_of(1, part.shape[0]),
        parts,
        nexts[:2],
        nexts[2:],
        pieces_third,
        fourth,
        update_rows,
        at_place + 1,
        plane,
    )
    fourth = [a, b, c, d]
    chunks, keep, send = tie((chunks, keep, send))

    part = reduce_chunks(chunks, plane, scalars)
    part, keep, send, y_fourth = tie((part, keep, send, y_fourth))
    pieces_fourth = with_x(x_fourth, own_fourth, y_fourth)
    halves_third = keep, permute(send, 1)
    part = (part.astype(F32) + permute(part, mask_z1).astype(F32)).astype(BF16)
    sibling = permute(part, mask_z2)
    part, sibling, pieces_fourth, halves_third = tie((part, sibling, pieces_fourth, halves_third))
    parts = spread_both(part, sibling)
    update, keep_fourth, send_fourth = solve_half(
        scalars,
        plan_of(2, part.shape[0]),
        parts,
        fourth[:2],
        fourth[2:],
        pieces_fourth,
        [],
        update_rows,
        0,
        [],
    )
    halves_fourth = keep_fourth, permute(send_fourth, 1)
    everywhere = ("z2", "z1", "x", "y")
    count = lax.axis_size(everywhere)
    arrived = lax.all_to_all(update, everywhere, 0, 0, tiled=True)
    solved_third, solved_fourth = join_columns(scalars, [halves_third, halves_fourth])
    arrived, solved_third, solved_fourth = tie((arrived, solved_third, solved_fourth))
    chunk = update_rows // count
    keep, send = kernel_call(
        functools.partial(core_split_kernel, count),
        [(aval(chunk // 2, half, F32), True)] * 2,
        scalars,
        [arrived],
        scratch=[pltpu.VMEM((chunk, half), F32)],
    )
    ancestor = join_columns(scalars, [(keep, permute(send, 1))])[0]
    return solved_first, solved_second, solved_third, solved_fourth, ancestor


def solution(mesh):
    n_leaf, n_rows = mesh.shape["leaf"], mesh.shape["rows"]
    fine = Mesh(mesh.devices.reshape(n_leaf // 8, 2, 2, 2, n_rows // 2, 2), AXES)
    rows, cols = P(AXES, None), P(None, AXES)
    return jax.shard_map(
        per_device,
        mesh=fine,
        in_specs=(rows,) * 8 + (cols,) * 4 + (P(),) * 3,
        out_specs=(rows,) * 5,
        check_vma=False,
    )
```

```python
import functools
import math

import jax
import jax.numpy as jnp
from jax import lax
from jax.experimental import pallas as pl
from jax.experimental.pallas import tpu as pltpu
from jax.sharding import Mesh
from jax.sharding import PartitionSpec as P

BF16 = jnp.bfloat16
F32 = jnp.float32
AXES = ("hi", "z2", "z1", "x", "y", "core")
PLANE = ("x", "y")
VMEM = pl.BlockSpec(memory_space=pltpu.VMEM)
SMEM = pl.BlockSpec(memory_space=pltpu.SMEM)
ANY = pl.BlockSpec(memory_space=pl.ANY)
MIB = 1 << 20


def permute(value, mask, upward=False):
    total = lax.axis_size(AXES)
    pairs = [(i, i ^ mask) for i in range(total) if not upward or (i ^ mask) > i]
    return lax.ppermute(value, AXES, pairs)


def row_tile(rows):
    return next(t for t in (512, 384, 256, 192, 128, 96, 64, 48, 32, 16) if rows % t == 0)


def aval(rows, cols, dtype):
    return jax.ShapeDtypeStruct((rows, cols), dtype)


def kernel_call(kernel, outs, scalars, vmem, hbm=(), scratch=(), limit=8):
    operands = [pltpu.with_memory_space_constraint(o, pltpu.VMEM) for o in vmem]
    return pl.pallas_call(
        kernel,
        out_shape=[pltpu.VMEM(o.shape, o.dtype) if inside else o for o, inside in outs],
        in_specs=[SMEM] + [VMEM] * len(vmem) + [ANY] * len(hbm),
        out_specs=[ANY if inside is False else VMEM for _, inside in outs],
        scratch_shapes=list(scratch),
        compiler_params=pltpu.CompilerParams(vmem_limit_bytes=limit * MIB),
        cost_estimate=pl.CostEstimate(flops=1, bytes_accessed=1, transcendentals=0),
    )(scalars, *operands, *[pltpu.with_memory_space_constraint(o, pltpu.HBM) for o in hbm])


def tiles(rows, step):
    tile = row_tile(rows)

    def body(i, carry):
        step(pl.ds(pl.multiple_of(i * tile, tile), tile))
        return carry

    lax.fori_loop(0, rows // tile, body, 0)


def dot(a, b):
    return jnp.dot(a, b, preferred_element_type=F32)


def start_all(sources, targets, sems):
    copies = [
        pltpu.make_async_copy(source, target, sems.at[i])
        for i, (source, target) in enumerate(zip(sources, targets))
    ]
    for copy in copies:
        copy.start()
    return copies


def near_kernel(scalars, b0, b1, inverse, panel, acc, far, panel_out, near, sems):
    rows, depth = inverse.shape[0], b0.shape[0]
    tile = row_tile(rows)
    n_far = far.shape[1] // depth
    columns = [
        pl.ds(pl.multiple_of(scalars[1 + i] * depth, depth), depth) for i in range(2 + n_far)
    ]
    sources, targets = [], []
    for i in range(rows // tile):
        at = pl.ds(i * tile, tile)
        for j in range(2):
            sources.append(inverse.at[at, columns[j]])
            targets.append(near.at[at, pl.ds(j * depth, depth)])
    for j in range(n_far):
        sources.append(inverse.at[:, columns[2 + j]])
        targets.append(far.at[:, pl.ds(j * depth, depth)])
    sources.append(panel)
    targets.append(panel_out)
    copies = start_all(sources, targets, sems)
    for i in range(rows // tile):
        at = pl.ds(i * tile, tile)
        copies[2 * i].wait()
        copies[2 * i + 1].wait()
        acc[at, :] = dot(near[at, :depth], b0[...]) + dot(near[at, depth:], b1[...])
    for copy in copies[2 * (rows // tile) :]:
        copy.wait()


def split_panel(core, panel, x_ref, keep, send):
    half = keep.shape[1]

    def step(at):
        part = dot(panel[at, :], x_ref[...])
        low, high = part[:, :half], part[:, half:]
        keep[at, :] = jnp.where(core == 0, low, high)
        send[at, :] = jnp.where(core == 0, high, low).astype(BF16)

    tiles(panel.shape[0], step)


def far_kernel(n_far, n_next, scalars, acc, panel, far, *refs):
    pieces, refs = refs[:n_far], refs[n_far:]
    solved, keep, send = refs[n_next : n_next + 3]
    x_ref, sem, sems = refs[-3:]
    copies = start_all(refs[:n_next], refs[n_next + 3 : -3], sems)
    depth = pieces[0].shape[0]

    def step(at):
        total = acc[at, :]
        for j, piece in enumerate(pieces):
            total += dot(far[at, j * depth : (j + 1) * depth], piece[...])
        x_ref[at, :] = total.astype(BF16)

    tiles(far.shape[0], step)
    result = pltpu.make_async_copy(x_ref, solved, sem)
    result.start()
    split_panel(scalars[0], panel, x_ref, keep, send)
    for copy in [*copies, result]:
        copy.wait()


def split_kernel(scalars, *refs):
    *arrays, keep, send, held, sems = refs
    core, half, first, targets = scalars[0], keep.shape[1], 0, []
    for array in arrays:
        targets.append(held.at[pl.ds(first, array.shape[0]), :])
        first += array.shape[0]
    for copy in start_all(arrays, targets, sems):
        copy.wait()
    low, high = held[:, :half], held[:, half:]
    keep[...] = jnp.where(core == 0, low, high)
    send[...] = jnp.where(core == 0, high, low)


def pack_kernel(groups, scalars, keep, received, *outs):
    core = scalars[0]
    for group, out in zip(groups, outs):
        at = 0
        for first, rows in group:
            for lane, part in ((core, keep), (1 - core, received)):
                target = pl.ds(pl.multiple_of(at + lane * rows, math.gcd(rows, 16)), rows)
                out[target, :] = part[first : first + rows, :]
            at += 2 * rows


def join_kernel(scalars, own, other, out):
    half = own.shape[1]
    out[:, :half] = jnp.where(scalars[0] == 0, own[...], other[...])
    out[:, half:] = jnp.where(scalars[0] == 0, other[...], own[...])


def join_all_kernel(scalars, *refs):
    count = len(refs) // 3
    for i in range(count):
        join_kernel(scalars, refs[2 * i], refs[2 * i + 1], refs[2 * count + i])


def join_columns(scalars, pairs):
    return kernel_call(
        join_all_kernel,
        [(aval(own.shape[0], 2 * own.shape[1], own.dtype), None) for own, _ in pairs],
        scalars,
        [v for pair in pairs for v in pair],
    )


def hand_out(place, value, own, sends):
    rows = own.shape[0]
    for mask, out in enumerate([own, *sends]):
        at = pl.ds(pl.multiple_of((place ^ mask) * rows, rows), rows)
        out[...] = value[at, :].astype(out.dtype)


def pair_sum_kernel(at_place, scalars, keep, received, own, *rest):
    *sends, total = rest
    total[...] = keep[...] + received[...].astype(F32)
    hand_out(scalars[at_place], total, own, sends)


def sum_kernel(scalars, own, *rest):
    total = own[...]
    for other in rest[:-1]:
        total += other[...].astype(F32)
    rest[-1][...] = total.astype(rest[-1].dtype)


def chunks_of(rows, cols, masks):
    rows //= len(masks)
    return [(aval(rows, cols, F32), True)] + [(aval(rows, cols, BF16), True)] * (len(masks) - 1)


def pair_sum(keep, send, scalars, at_place, masks):
    received = permute(send, 1)
    return kernel_call(
        functools.partial(pair_sum_kernel, at_place),
        chunks_of(*keep.shape, masks),
        scalars,
        [keep, received],
        scratch=[pltpu.VMEM(keep.shape, F32)],
    )


def reduce_chunks(chunks, masks, scalars):
    own, *sends = chunks
    arrived = [permute(value, mask) for value, mask in zip(sends, masks[1:])]
    return kernel_call(
        sum_kernel, [(aval(*own.shape, BF16), True)], scalars, [own, *arrived]
    )[0]


def core_split_kernel(count, scalars, chunks, keep, send, total):
    rows = total.shape[0]
    value = chunks[:rows, :].astype(F32)
    for i in range(1, count):
        value += chunks[i * rows : (i + 1) * rows, :].astype(F32)
    total[...] = value
    rows = keep.shape[0]
    keep[...] = total[pl.ds(pl.multiple_of(scalars[0] * rows, 8), rows), :]
    send[...] = total[pl.ds(pl.multiple_of((1 - scalars[0]) * rows, 8), rows), :]


def start_loads(scalars, at_order, size, pieces, ready, lanes, sems, first):
    copies = []
    for piece in pieces:
        for row in range(0, piece.shape[0], size):
            i = len(copies)
            at = pl.multiple_of(scalars[at_order + i] * size, size)
            target = ready.at[pl.ds(at, size), lanes]
            copies.append(
                pltpu.make_async_copy(piece.at[pl.ds(row, size), :], target, sems.at[first + i])
            )
    for copy in copies:
        copy.start()
    return copies


def subtract_updates(scalars, plan, update, ready, lanes):
    unit, places, block, at_table = plan[:4]
    for i, (index, row) in enumerate(places):
        at = pl.ds(pl.multiple_of(scalars[at_table + index] * block + row, unit), unit)
        value = update[i * unit : (i + 1) * unit, :].astype(F32)
        ready[at, lanes] = (ready[at, lanes].astype(F32) - value).astype(BF16)


def subtract_parts(scalars, plan, parts, ready, lanes):
    unit, (width, at_place), block, at_table = plan[:4]
    chunk = parts[0].shape[0] // 2
    for mask, part in enumerate(parts):
        first = (scalars[at_place] ^ mask) * chunk
        for child in range(2):
            for start in range(0, chunk, unit):
                row = first + start
                index = scalars[at_table + child * width + lax.div(row, block)]
                at = pl.ds(pl.multiple_of(index * block + lax.rem(row, block), unit), unit)
                value = part[pl.ds(child * chunk + start, unit), :].astype(F32)
                ready[at, lanes] = (ready[at, lanes].astype(F32) - value).astype(BF16)


def whole_kernel(plan, scalars, mine, other, inverse, panel, *refs):
    at_order, size, n_pieces, n_next = plan[4:]
    pieces, refs = refs[: 2 * n_pieces], refs[2 * n_pieces :]
    nexts, (solved, keep, send) = refs[:n_next], refs[n_next : n_next + 3]
    ready, x_ref, load_sems, sem, sems = refs[-5:]
    core, half = scalars[0], keep.shape[1]
    lanes = [pl.ds(pl.multiple_of(c * half, half), half) for c in (core, 1 - core)]
    runs = load_sems.shape[0] // 2
    arriving = []
    for i in range(2):
        part = pieces[i * n_pieces : (i + 1) * n_pieces]
        arriving += start_loads(
            scalars, at_order + i * runs, size, part, ready, lanes[i], load_sems, i * runs
        )
    for copy in arriving:
        copy.wait()
    copies = start_all(nexts, refs[n_next + 3 : -5], sems)
    subtract_updates(scalars, plan, mine, ready, lanes[0])
    subtract_updates(scalars, plan, other, ready, lanes[1])

    def step(at):
        x_ref[at, :] = dot(inverse[at, :], ready[...]).astype(BF16)

    tiles(inverse.shape[0], step)
    result = pltpu.make_async_copy(x_ref, solved, sem)
    result.start()
    split_panel(core, panel, x_ref, keep, send)
    for copy in [*copies, result]:
        copy.wait()


def half_kernel(plan, turned, at_place, n_chunks, n_parts, scalars, *refs):
    parts, refs = refs[:n_parts], refs[n_parts:]
    (inverse_a, inverse_b, panel_a, panel_b), refs = refs[:4], refs[4:]
    at_order, size, n_pieces, n_next = plan[4:]
    pieces, refs = refs[:n_pieces], refs[n_pieces:]
    nexts, refs = refs[:n_next], refs[n_next:]
    chunks, (x_keep, x_send) = refs[:n_chunks], refs[n_chunks : n_chunks + 2]
    ready, update, load_sems, sems = refs[-4:]
    lanes = pl.ds(0, parts[0].shape[1])
    arriving = start_loads(scalars, at_order, size, pieces, ready, lanes, load_sems, 0)
    for copy in arriving:
        copy.wait()
    copies = start_all(nexts, refs[n_chunks + 2 : -4], sems)
    subtract_parts(scalars, plan, parts, ready, lanes)

    def step(at):
        x_keep[at, :] = dot(inverse_a[at, :], ready[...]).astype(BF16)
        x_send[at, :] = dot(inverse_b[at, :], ready[...]).astype(BF16)

    tiles(inverse_a.shape[0], step)

    def panel_step(at):
        if turned:
            dims = (((0,), (0,)), ((), ()))
            part = lax.dot_general(panel_a[:, at], x_keep[...], dims, preferred_element_type=F32)
            part += lax.dot_general(panel_b[:, at], x_send[...], dims, preferred_element_type=F32)
        else:
            part = dot(panel_a[at, :], x_keep[...]) + dot(panel_b[at, :], x_send[...])
        update[at, :] = part.astype(update.dtype)

    tiles(update.shape[0], panel_step)
    if n_chunks > 1:
        hand_out(scalars[at_place], update, chunks[0], chunks[1:])
    else:
        chunks[0][...] = update[...].astype(BF16)
    for copy in copies:
        copy.wait()


def in_vmem(arrays):
    return [(aval(*v.shape, BF16), True) for v in arrays]


def solve_whole(scalars, plan, mine, other, inverse, panel, pieces, nexts):
    (rows, depth), half = inverse.shape, mine.shape[1]
    outs = [(aval(rows, 2 * half, BF16), False)]
    outs += [(aval(panel.shape[0], half, t), True) for t in (F32, BF16)]
    return kernel_call(
        functools.partial(whole_kernel, plan),
        outs + in_vmem(nexts),
        scalars,
        [mine, other, inverse, panel],
        [*pieces, *nexts],
        [
            pltpu.VMEM((depth, 2 * half), BF16),
            pltpu.VMEM((rows, 2 * half), BF16),
            pltpu.SemaphoreType.DMA((2 * depth // plan[5],)),
            pltpu.SemaphoreType.DMA,
            pltpu.SemaphoreType.DMA((max(1, len(nexts)),)),
        ],
        limit=14,
    )


def solve_half(scalars, plan, parts, inverses, panels, pieces, nexts, update_rows, at_place, masks):
    (rows, depth), half = inverses[0].shape, parts[0].shape[1]
    chunks = chunks_of(update_rows, half, masks) if masks else [(aval(update_rows, half, BF16), True)]
    outs = chunks + [(aval(rows, half, BF16), True)] * 2
    turned = panels[0].shape[0] != update_rows
    return kernel_call(
        functools.partial(half_kernel, plan, turned, at_place, len(chunks), len(parts)),
        outs + in_vmem(nexts),
        scalars,
        [*parts, *inverses, *panels],
        [*pieces, *nexts],
        [
            pltpu.VMEM((depth, half), BF16),
            pltpu.VMEM((update_rows, half), F32),
            pltpu.SemaphoreType.DMA((depth // plan[5],)),
            pltpu.SemaphoreType.DMA((max(1, len(nexts)),)),
        ],
        limit=12,
    )


def per_device(
    loads_first,
    loads_second,
    loads_third,
    loads_fourth,
    inverse_first,
    inverse_second,
    inverse_third,
    inverse_fourth,
    panel_first,
    panel_second,
    panel_third,
    panel_fourth,
    blocks_first,
    blocks_second,
    blocks_third,
):
    n_y, n_rows = lax.axis_size("y"), 2 * lax.axis_size("y")
    core, x_index, y_index = (lax.axis_index(a) for a in ("core", "x", "y"))
    z1, z2 = lax.axis_index("z1"), lax.axis_index("z2")
    row_index = y_index * 2 + core
    z_index = z2 * 2 + z1
    leaf = (lax.axis_index("hi") * 4 + z_index) * 2 + x_index
    mask_x, mask_z1, mask_z2 = n_rows, 2 * n_rows, 4 * n_rows
    y_masks = [2 * y for y in range(1, n_y)]
    plane_masks = [(x, y) for y in range(n_y) for x in range(2)]
    update_rows, width = panel_first.shape[0], blocks_first.shape[1]
    block = update_rows // width
    rows, depth = inverse_first.shape[0], loads_first.shape[0]
    cols = loads_first.shape[1]
    half = cols // 2

    values = [core, row_index, row_index ^ 1]
    for mask in y_masks:
        values += [row_index ^ mask, row_index ^ mask ^ 1]
    at_place = len(values)
    values += [y_index, x_index * n_y + y_index]
    column = [0, *y_masks]
    plane = [x * mask_x + y * 2 for x in range(2) for y in range(n_y)]
    at_order = []
    for planes in ([0], [z1, z1 ^ 1], [z_index, z_index ^ 2, z_index ^ 1, z_index ^ 3]):
        at_order.append(len(values))
        for _ in range(2 if len(planes) == 1 else 1):
            for x, y in plane_masks:
                place = (x_index ^ x) * n_y + (y_index ^ y)
                values += [z * n_rows + place for z in planes]
    at_table = [len(values) + 2 * width * i for i in range(3)]
    children = [(leaf >> 1) * 2, (leaf >> 1) * 2 + 1]
    parts = [jnp.stack([jnp.asarray(v, jnp.int32) for v in values])]
    for table, pair in (
        (blocks_first, children),
        (blocks_second, [leaf >> 1, (leaf >> 1) ^ 1]),
        (blocks_third, [leaf >> 2, (leaf >> 2) ^ 1]),
    ):
        parts += [lax.dynamic_index_in_dim(table, c, 0, keepdims=False) for c in pair]
    scalars = jnp.concatenate(parts)

    tie = lax.optimization_barrier

    n_far = 2 * len(y_masks)
    sibling = permute(loads_first, 1)
    shards = [permute(loads_first, mask, upward=True) for mask in y_masks]
    loads = [loads_second, loads_third, loads_fourth]
    sizes = [v.shape[0] for v in loads]
    keep, send = kernel_call(
        split_kernel,
        [(aval(sum(sizes), half, BF16), True)] * 2,
        core[None].astype(jnp.int32),
        [],
        loads,
        [pltpu.VMEM((sum(sizes), cols), BF16), pltpu.SemaphoreType.DMA((len(loads),))],
    )
    received = permute(send, 1)
    scalars, keep, received, sibling, inverse_third = tie(
        (scalars, keep, received, sibling, inverse_third)
    )
    inverses = inverse_third, permute(inverse_third, 1)
    acc, far, panel = kernel_call(
        near_kernel,
        [
            (aval(rows, cols, F32), True),
            (aval(rows, n_far * depth, BF16), True),
            (aval(*panel_first.shape, BF16), True),
        ],
        scalars,
        [loads_first, sibling],
        [inverse_first, panel_first],
        [
            pltpu.VMEM((rows, 2 * depth), BF16),
            pltpu.SemaphoreType.DMA((2 * (rows // row_tile(rows)) + n_far + 1,)),
        ],
        limit=16,
    )
    runs = [(sum(sizes[:i]), n) for i, n in enumerate(sizes)]
    groups = [[run] for run in runs]
    own_second, half_third, half_fourth = kernel_call(
        functools.partial(pack_kernel, groups),
        [(aval(2 * sum(n for _, n in group), half, BF16), True) for group in groups],
        scalars,
        [keep, received],
    )
    x_second = permute(own_second, mask_x)
    by_z2 = permute(half_fourth, mask_z2)
    by_z1 = permute(half_third, mask_z1)
    acc, by_z1, by_z2 = tie((acc, by_z1, by_z2))
    own_third = jnp.concatenate([half_third, by_z1], 0)
    half_fourth = jnp.concatenate([half_fourth, by_z2], 0)
    x_third = permute(own_third, mask_x)
    by_z1 = permute(half_fourth, mask_z1)
    shards, acc, far, panel, own_second, x_second, inverses = tie(
        (shards, acc, far, panel, own_second, x_second, inverses)
    )

    pieces = [v for shard in shards for v in (shard, permute(shard, 1))]
    y_second = [permute(own_second, mask) for mask in y_masks]
    nexts = [inverse_second, panel_second]
    solved_first, keep, send, inverse_second, panel_second = kernel_call(
        functools.partial(far_kernel, n_far, len(nexts)),
        [
            (aval(rows, cols, BF16), False),
            (aval(update_rows, half, F32), True),
            (aval(update_rows, half, BF16), True),
        ]
        + in_vmem(nexts),
        scalars,
        [acc, panel, far, *pieces],
        nexts,
        [
            pltpu.VMEM((rows, cols), BF16),
            pltpu.SemaphoreType.DMA,
            pltpu.SemaphoreType.DMA((len(nexts),)),
        ],
    )
    keep, send, y_second, by_z1, x_third = tie((keep, send, y_second, by_z1, x_third))
    chunks = pair_sum(keep, send, scalars, at_place, column)
    chunks, panel_third = tie((chunks, panel_third))
    panels = panel_third, permute(panel_third, 1)

    def with_x(x_piece, own, y_pieces):
        pieces = [own, x_piece]
        for piece in y_pieces:
            pieces += [piece, permute(piece, mask_x)]
        return pieces

    pieces_second = with_x(x_second, own_second, y_second)
    early = [own_second, x_second, *y_second]
    across_early = [permute(piece, 1) for piece in early]
    own_fourth = jnp.concatenate([half_fourth, by_z1], 0)
    part = reduce_chunks(chunks, column, scalars)
    part, pieces_second, across_early, own_third, own_fourth = tie(
        (part, pieces_second, across_early, own_third, own_fourth)
    )

    def spread(value):
        return lax.all_gather(value, PLANE, axis=0, tiled=True)

    def spread_both(own, sib):
        both = jnp.concatenate([own, sib], 0)
        return [both] + [permute(both, mask) for mask in plane[1:]]

    def plan_of(level, chunk):
        unit = math.gcd(chunk, block)
        places = width, at_place + 1
        if level == 0:
            rows = [divmod(row, block) for row in range(0, update_rows, unit)]
            places = [(child * width + i, row) for child in range(2) for i, row in rows]
        n_next = 4 if level < 2 else 0
        return unit, places, block, at_table[level], at_order[level], 2 * sizes[level], n_pieces, n_next

    n_pieces = len(plane_masks)

    across = across_early[:2]
    for i in range(len(y_masks)):
        across += [across_early[2 + i], permute(pieces_second[3 + 2 * i], 1)]
    pieces_second += across
    mine = spread(part)
    mine, pieces_second, own_third, own_fourth = tie(
        (mine, pieces_second, own_third, own_fourth)
    )
    other = permute(mine, 1)
    x_fourth = permute(own_fourth, mask_x)
    y_third = [permute(own_third, mask) for mask in y_masks]
    solved_second, keep, send, *nexts = solve_whole(
        scalars,
        plan_of(0, part.shape[0]),
        mine,
        other,
        inverse_second,
        panel_second,
        pieces_second,
        [*inverses, *panels],
    )
    keep, send, x_fourth, y_third = tie((keep, send, x_fourth, y_third))

    chunks = pair_sum(keep, send, scalars, at_place + 1, plane)
    chunks, inverse_fourth, panel_fourth = tie((chunks, inverse_fourth, panel_fourth))
    part = reduce_chunks(chunks, plane, scalars)
    part, own_fourth = tie((part, own_fourth))
    sibling = permute(part, mask_z1)
    pieces_third = with_x(x_third, own_third, y_third)
    y_fourth = [permute(own_fourth, mask) for mask in y_masks]
    panel_fourth = panel_fourth.T
    fourth = [
        inverse_fourth, permute(inverse_fourth, 1), panel_fourth, permute(panel_fourth, 1),
    ]
    part, sibling, pieces_third, fourth, y_fourth = tie(
        (part, sibling, pieces_third, fourth, y_fourth)
    )
    parts = spread_both(part, sibling)
    *chunks, keep, send, a, b, c, d = solve_half(
        scalars,
        plan_of(1, part.shape[0]),
        parts,
        nexts[:2],
        nexts[2:],
        pieces_third,
        fourth,
        update_rows,
        at_place + 1,
        plane,
    )
    fourth = [a, b, c, d]
    chunks, keep, send = tie((chunks, keep, send))

    part = reduce_chunks(chunks, plane, scalars)
    part, keep, send, y_fourth = tie((part, keep, send, y_fourth))
    pieces_fourth = with_x(x_fourth, own_fourth, y_fourth)
    halves_third = keep, permute(send, 1)
    part = (part.astype(F32) + permute(part, mask_z1).astype(F32)).astype(BF16)
    sibling = permute(part, mask_z2)
    part, sibling, pieces_fourth, halves_third = tie((part, sibling, pieces_fourth, halves_third))
    parts = spread_both(part, sibling)
    update, keep_fourth, send_fourth = solve_half(
        scalars,
        plan_of(2, part.shape[0]),
        parts,
        fourth[:2],
        fourth[2:],
        pieces_fourth,
        [],
        update_rows,
        0,
        [],
    )
    halves_fourth = keep_fourth, permute(send_fourth, 1)
    everywhere = ("z2", "z1", "x", "y")
    count = lax.axis_size(everywhere)
    arrived = lax.all_to_all(update, everywhere, 0, 0, tiled=True)
    solved_third, solved_fourth = join_columns(scalars, [halves_third, halves_fourth])
    arrived, solved_third, solved_fourth = tie((arrived, solved_third, solved_fourth))
    chunk = update_rows // count
    keep, send = kernel_call(
        functools.partial(core_split_kernel, count),
        [(aval(chunk // 2, half, F32), True)] * 2,
        scalars,
        [arrived],
        scratch=[pltpu.VMEM((chunk, half), F32)],
    )
    ancestor = join_columns(scalars, [(keep, permute(send, 1))])[0]
    return solved_first, solved_second, solved_third, solved_fourth, ancestor


def solution(mesh):
    n_leaf, n_rows = mesh.shape["leaf"], mesh.shape["rows"]
    fine = Mesh(mesh.devices.reshape(n_leaf // 8, 2, 2, 2, n_rows // 2, 2), AXES)
    rows, cols = P(AXES, None), P(None, AXES)
    return jax.shard_map(
        per_device,
        mesh=fine,
        in_specs=(rows,) * 8 + (cols,) * 4 + (P(),) * 3,
        out_specs=(rows,) * 5,
        check_vma=False,
    )
```

```python
import functools
import math

import jax
import jax.numpy as jnp
from jax import lax
from jax.experimental import pallas as pl
from jax.experimental.pallas import tpu as pltpu
from jax.sharding import Mesh
from jax.sharding import PartitionSpec as P

BF16 = jnp.bfloat16
F32 = jnp.float32
AXES = ("hi", "z2", "z1", "x", "y", "core")
PLANE = ("x", "y")
VMEM = pl.BlockSpec(memory_space=pltpu.VMEM)
SMEM = pl.BlockSpec(memory_space=pltpu.SMEM)
ANY = pl.BlockSpec(memory_space=pl.ANY)
MIB = 1 << 20


def permute(value, mask, upward=False):
    total = lax.axis_size(AXES)
    pairs = [(i, i ^ mask) for i in range(total) if not upward or (i ^ mask) > i]
    return lax.ppermute(value, AXES, pairs)


def row_tile(rows):
    return next(t for t in (512, 384, 256, 192, 128, 96, 64, 48, 32, 16) if rows % t == 0)


def aval(rows, cols, dtype):
    return jax.ShapeDtypeStruct((rows, cols), dtype)


def kernel_call(kernel, outs, scalars, vmem, hbm=(), scratch=(), limit=8):
    operands = [pltpu.with_memory_space_constraint(o, pltpu.VMEM) for o in vmem]
    return pl.pallas_call(
        kernel,
        out_shape=[pltpu.VMEM(o.shape, o.dtype) if inside else o for o, inside in outs],
        in_specs=[SMEM] + [VMEM] * len(vmem) + [ANY] * len(hbm),
        out_specs=[ANY if inside is False else VMEM for _, inside in outs],
        scratch_shapes=list(scratch),
        compiler_params=pltpu.CompilerParams(vmem_limit_bytes=limit * MIB),
        cost_estimate=pl.CostEstimate(flops=1, bytes_accessed=1, transcendentals=0),
    )(scalars, *operands, *[pltpu.with_memory_space_constraint(o, pltpu.HBM) for o in hbm])


def tiles(rows, step):
    tile = row_tile(rows)

    def body(i, carry):
        step(pl.ds(pl.multiple_of(i * tile, tile), tile))
        return carry

    lax.fori_loop(0, rows // tile, body, 0)


def dot(a, b):
    return jnp.dot(a, b, preferred_element_type=F32)


def start_all(sources, targets, sems):
    copies = [
        pltpu.make_async_copy(source, target, sems.at[i])
        for i, (source, target) in enumerate(zip(sources, targets))
    ]
    for copy in copies:
        copy.start()
    return copies


def near_kernel(scalars, b0, b1, inverse, panel, acc, far, panel_out, near, sems):
    rows, depth = inverse.shape[0], b0.shape[0]
    tile = row_tile(rows)
    n_far = far.shape[1] // depth
    columns = [
        pl.ds(pl.multiple_of(scalars[1 + i] * depth, depth), depth) for i in range(2 + n_far)
    ]
    sources, targets = [], []
    for i in range(rows // tile):
        at = pl.ds(i * tile, tile)
        for j in range(2):
            sources.append(inverse.at[at, columns[j]])
            targets.append(near.at[at, pl.ds(j * depth, depth)])
    for j in range(n_far):
        sources.append(inverse.at[:, columns[2 + j]])
        targets.append(far.at[:, pl.ds(j * depth, depth)])
    sources.append(panel)
    targets.append(panel_out)
    copies = start_all(sources, targets, sems)
    for i in range(rows // tile):
        at = pl.ds(i * tile, tile)
        copies[2 * i].wait()
        copies[2 * i + 1].wait()
        acc[at, :] = dot(near[at, :depth], b0[...]) + dot(near[at, depth:], b1[...])
    for copy in copies[2 * (rows // tile) :]:
        copy.wait()


def split_panel(core, panel, x_ref, keep, send):
    half = keep.shape[1]

    def step(at):
        part = dot(panel[at, :], x_ref[...])
        low, high = part[:, :half], part[:, half:]
        keep[at, :] = jnp.where(core == 0, low, high)
        send[at, :] = jnp.where(core == 0, high, low).astype(BF16)

    tiles(panel.shape[0], step)


def far_kernel(n_far, n_next, scalars, acc, panel, far, *refs):
    pieces, refs = refs[:n_far], refs[n_far:]
    solved, keep, send = refs[n_next : n_next + 3]
    x_ref, sem, sems = refs[-3:]
    copies = start_all(refs[:n_next], refs[n_next + 3 : -3], sems)
    depth = pieces[0].shape[0]

    def step(at):
        total = acc[at, :]
        for j, piece in enumerate(pieces):
            total += dot(far[at, j * depth : (j + 1) * depth], piece[...])
        x_ref[at, :] = total.astype(BF16)

    tiles(far.shape[0], step)
    result = pltpu.make_async_copy(x_ref, solved, sem)
    result.start()
    split_panel(scalars[0], panel, x_ref, keep, send)
    for copy in [*copies, result]:
        copy.wait()


def split_kernel(scalars, *refs):
    *arrays, keep, send, held, sems = refs
    core, half, first, targets = scalars[0], keep.shape[1], 0, []
    for array in arrays:
        targets.append(held.at[pl.ds(first, array.shape[0]), :])
        first += array.shape[0]
    for copy in start_all(arrays, targets, sems):
        copy.wait()
    low, high = held[:, :half], held[:, half:]
    keep[...] = jnp.where(core == 0, low, high)
    send[...] = jnp.where(core == 0, high, low)


def pack_kernel(groups, scalars, keep, received, *outs):
    core = scalars[0]
    for group, out in zip(groups, outs):
        at = 0
        for first, rows in group:
            for lane, part in ((core, keep), (1 - core, received)):
                target = pl.ds(pl.multiple_of(at + lane * rows, math.gcd(rows, 16)), rows)
                out[target, :] = part[first : first + rows, :]
            at += 2 * rows


def join_kernel(scalars, own, other, out):
    half = own.shape[1]
    out[:, :half] = jnp.where(scalars[0] == 0, own[...], other[...])
    out[:, half:] = jnp.where(scalars[0] == 0, other[...], own[...])


def join_all_kernel(scalars, *refs):
    count = len(refs) // 3
    for i in range(count):
        join_kernel(scalars, refs[2 * i], refs[2 * i + 1], refs[2 * count + i])


def join_columns(scalars, pairs):
    return kernel_call(
        join_all_kernel,
        [(aval(own.shape[0], 2 * own.shape[1], own.dtype), None) for own, _ in pairs],
        scalars,
        [v for pair in pairs for v in pair],
    )


def hand_out(place, value, own, sends):
    rows = own.shape[0]
    for mask, out in enumerate([own, *sends]):
        at = pl.ds(pl.multiple_of((place ^ mask) * rows, rows), rows)
        out[...] = value[at, :].astype(out.dtype)


def pair_sum_kernel(at_place, scalars, keep, received, own, *rest):
    *sends, total = rest
    total[...] = keep[...] + received[...].astype(F32)
    hand_out(scalars[at_place], total, own, sends)


def sum_kernel(scalars, own, *rest):
    total = own[...]
    for other in rest[:-1]:
        total += other[...].astype(F32)
    rest[-1][...] = total.astype(rest[-1].dtype)


def chunks_of(rows, cols, masks):
    rows //= len(masks)
    return [(aval(rows, cols, F32), True)] + [(aval(rows, cols, BF16), True)] * (len(masks) - 1)


def pair_sum(keep, send, scalars, at_place, masks):
    received = permute(send, 1)
    return kernel_call(
        functools.partial(pair_sum_kernel, at_place),
        chunks_of(*keep.shape, masks),
        scalars,
        [keep, received],
        scratch=[pltpu.VMEM(keep.shape, F32)],
    )


def reduce_chunks(chunks, masks, scalars):
    own, *sends = chunks
    arrived = [permute(value, mask) for value, mask in zip(sends, masks[1:])]
    return kernel_call(
        sum_kernel, [(aval(*own.shape, BF16), True)], scalars, [own, *arrived]
    )[0]


def core_split_kernel(count, scalars, chunks, keep, send, total):
    rows = total.shape[0]
    value = chunks[:rows, :].astype(F32)
    for i in range(1, count):
        value += chunks[i * rows : (i + 1) * rows, :].astype(F32)
    total[...] = value
    rows = keep.shape[0]
    keep[...] = total[pl.ds(pl.multiple_of(scalars[0] * rows, 8), rows), :]
    send[...] = total[pl.ds(pl.multiple_of((1 - scalars[0]) * rows, 8), rows), :]


def start_loads(scalars, at_order, size, pieces, ready, lanes, sems, first):
    copies = []
    for piece in pieces:
        for row in range(0, piece.shape[0], size):
            i = len(copies)
            at = pl.multiple_of(scalars[at_order + i] * size, size)
            target = ready.at[pl.ds(at, size), lanes]
            copies.append(
                pltpu.make_async_copy(piece.at[pl.ds(row, size), :], target, sems.at[first + i])
            )
    for copy in copies:
        copy.start()
    return copies


def subtract_updates(scalars, plan, update, ready, lanes):
    unit, places, block, at_table = plan[:4]
    for i, (index, row) in enumerate(places):
        at = pl.ds(pl.multiple_of(scalars[at_table + index] * block + row, unit), unit)
        value = update[i * unit : (i + 1) * unit, :].astype(F32)
        ready[at, lanes] = (ready[at, lanes].astype(F32) - value).astype(BF16)


def subtract_parts(scalars, plan, parts, ready, lanes):
    unit, (width, at_place), block, at_table = plan[:4]
    chunk = parts[0].shape[0] // 2
    for mask, part in enumerate(parts):
        first = (scalars[at_place] ^ mask) * chunk
        for child in range(2):
            for start in range(0, chunk, unit):
                row = first + start
                index = scalars[at_table + child * width + lax.div(row, block)]
                at = pl.ds(pl.multiple_of(index * block + lax.rem(row, block), unit), unit)
                value = part[pl.ds(child * chunk + start, unit), :].astype(F32)
                ready[at, lanes] = (ready[at, lanes].astype(F32) - value).astype(BF16)


def whole_kernel(plan, scalars, mine, other, inverse, panel, *refs):
    at_order, size, n_pieces, n_next = plan[4:]
    pieces, refs = refs[: 2 * n_pieces], refs[2 * n_pieces :]
    nexts, (solved, keep, send) = refs[:n_next], refs[n_next : n_next + 3]
    ready, x_ref, load_sems, sem, sems = refs[-5:]
    core, half = scalars[0], keep.shape[1]
    lanes = [pl.ds(pl.multiple_of(c * half, half), half) for c in (core, 1 - core)]
    runs = load_sems.shape[0] // 2
    arriving = []
    for i in range(2):
        part = pieces[i * n_pieces : (i + 1) * n_pieces]
        arriving += start_loads(
            scalars, at_order + i * runs, size, part, ready, lanes[i], load_sems, i * runs
        )
    for copy in arriving:
        copy.wait()
    copies = start_all(nexts, refs[n_next + 3 : -5], sems)
    subtract_updates(scalars, plan, mine, ready, lanes[0])
    subtract_updates(scalars, plan, other, ready, lanes[1])

    def step(at):
        x_ref[at, :] = dot(inverse[at, :], ready[...]).astype(BF16)

    tiles(inverse.shape[0], step)
    result = pltpu.make_async_copy(x_ref, solved, sem)
    result.start()
    split_panel(core, panel, x_ref, keep, send)
    for copy in [*copies, result]:
        copy.wait()


def half_kernel(plan, turned, at_place, n_chunks, n_parts, scalars, *refs):
    parts, refs = refs[:n_parts], refs[n_parts:]
    (inverse_a, inverse_b, panel_a, panel_b), refs = refs[:4], refs[4:]
    at_order, size, n_pieces, n_next = plan[4:]
    pieces, refs = refs[:n_pieces], refs[n_pieces:]
    nexts, refs = refs[:n_next], refs[n_next:]
    chunks, (x_keep, x_send) = refs[:n_chunks], refs[n_chunks : n_chunks + 2]
    ready, update, load_sems, sems = refs[-4:]
    lanes = pl.ds(0, parts[0].shape[1])
    arriving = start_loads(scalars, at_order, size, pieces, ready, lanes, load_sems, 0)
    for copy in arriving:
        copy.wait()
    copies = start_all(nexts, refs[n_chunks + 2 : -4], sems)
    subtract_parts(scalars, plan, parts, ready, lanes)

    def step(at):
        x_keep[at, :] = dot(inverse_a[at, :], ready[...]).astype(BF16)
        x_send[at, :] = dot(inverse_b[at, :], ready[...]).astype(BF16)

    tiles(inverse_a.shape[0], step)

    def panel_step(at):
        if turned:
            dims = (((0,), (0,)), ((), ()))
            part = lax.dot_general(panel_a[:, at], x_keep[...], dims, preferred_element_type=F32)
            part += lax.dot_general(panel_b[:, at], x_send[...], dims, preferred_element_type=F32)
        else:
            part = dot(panel_a[at, :], x_keep[...]) + dot(panel_b[at, :], x_send[...])
        update[at, :] = part.astype(update.dtype)

    tiles(update.shape[0], panel_step)
    if n_chunks > 1:
        hand_out(scalars[at_place], update, chunks[0], chunks[1:])
    else:
        chunks[0][...] = update[...].astype(BF16)
    for copy in copies:
        copy.wait()


def in_vmem(arrays):
    return [(aval(*v.shape, BF16), True) for v in arrays]


def solve_whole(scalars, plan, mine, other, inverse, panel, pieces, nexts):
    (rows, depth), half = inverse.shape, mine.shape[1]
    outs = [(aval(rows, 2 * half, BF16), False)]
    outs += [(aval(panel.shape[0], half, t), True) for t in (F32, BF16)]
    return kernel_call(
        functools.partial(whole_kernel, plan),
        outs + in_vmem(nexts),
        scalars,
        [mine, other, inverse, panel],
        [*pieces, *nexts],
        [
            pltpu.VMEM((depth, 2 * half), BF16),
            pltpu.VMEM((rows, 2 * half), BF16),
            pltpu.SemaphoreType.DMA((2 * depth // plan[5],)),
            pltpu.SemaphoreType.DMA,
            pltpu.SemaphoreType.DMA((max(1, len(nexts)),)),
        ],
        limit=14,
    )


def solve_half(scalars, plan, parts, inverses, panels, pieces, nexts, update_rows, at_place, masks):
    (rows, depth), half = inverses[0].shape, parts[0].shape[1]
    chunks = chunks_of(update_rows, half, masks) if masks else [(aval(update_rows, half, BF16), True)]
    outs = chunks + [(aval(rows, half, BF16), True)] * 2
    turned = panels[0].shape[0] != update_rows
    return kernel_call(
        functools.partial(half_kernel, plan, turned, at_place, len(chunks), len(parts)),
        outs + in_vmem(nexts),
        scalars,
        [*parts, *inverses, *panels],
        [*pieces, *nexts],
        [
            pltpu.VMEM((depth, half), BF16),
            pltpu.VMEM((update_rows, half), F32),
            pltpu.SemaphoreType.DMA((depth // plan[5],)),
            pltpu.SemaphoreType.DMA((max(1, len(nexts)),)),
        ],
        limit=12,
    )


def per_device(
    loads_first,
    loads_second,
    loads_third,
    loads_fourth,
    inverse_first,
    inverse_second,
    inverse_third,
    inverse_fourth,
    panel_first,
    panel_second,
    panel_third,
    panel_fourth,
    blocks_first,
    blocks_second,
    blocks_third,
):
    n_y, n_rows = lax.axis_size("y"), 2 * lax.axis_size("y")
    core, x_index, y_index = (lax.axis_index(a) for a in ("core", "x", "y"))
    z1, z2 = lax.axis_index("z1"), lax.axis_index("z2")
    row_index = y_index * 2 + core
    z_index = z2 * 2 + z1
    leaf = (lax.axis_index("hi") * 4 + z_index) * 2 + x_index
    mask_x, mask_z1, mask_z2 = n_rows, 2 * n_rows, 4 * n_rows
    y_masks = [2 * y for y in range(1, n_y)]
    plane_masks = [(x, y) for y in range(n_y) for x in range(2)]
    update_rows, width = panel_first.shape[0], blocks_first.shape[1]
    block = update_rows // width
    rows, depth = inverse_first.shape[0], loads_first.shape[0]
    cols = loads_first.shape[1]
    half = cols // 2

    values = [core, row_index, row_index ^ 1]
    for mask in y_masks:
        values += [row_index ^ mask, row_index ^ mask ^ 1]
    at_place = len(values)
    values += [y_index, x_index * n_y + y_index]
    column = [0, *y_masks]
    plane = [x * mask_x + y * 2 for x in range(2) for y in range(n_y)]
    at_order = []
    for planes in ([0], [z1, z1 ^ 1], [z_index, z_index ^ 2, z_index ^ 1, z_index ^ 3]):
        at_order.append(len(values))
        for _ in range(2 if len(planes) == 1 else 1):
            for x, y in plane_masks:
                place = (x_index ^ x) * n_y + (y_index ^ y)
                values += [z * n_rows + place for z in planes]
    at_table = [len(values) + 2 * width * i for i in range(3)]
    children = [(leaf >> 1) * 2, (leaf >> 1) * 2 + 1]
    parts = [jnp.stack([jnp.asarray(v, jnp.int32) for v in values])]
    for table, pair in (
        (blocks_first, children),
        (blocks_second, [leaf >> 1, (leaf >> 1) ^ 1]),
        (blocks_third, [leaf >> 2, (leaf >> 2) ^ 1]),
    ):
        parts += [lax.dynamic_index_in_dim(table, c, 0, keepdims=False) for c in pair]
    scalars = jnp.concatenate(parts)

    tie = lax.optimization_barrier

    n_far = 2 * len(y_masks)
    sibling = permute(loads_first, 1)
    shards = [permute(loads_first, mask, upward=True) for mask in y_masks]
    loads = [loads_second, loads_third, loads_fourth]
    sizes = [v.shape[0] for v in loads]
    keep, send = kernel_call(
        split_kernel,
        [(aval(sum(sizes), half, BF16), True)] * 2,
        core[None].astype(jnp.int32),
        [],
        loads,
        [pltpu.VMEM((sum(sizes), cols), BF16), pltpu.SemaphoreType.DMA((len(loads),))],
    )
    received = permute(send, 1)
    scalars, keep, received, sibling, inverse_third = tie(
        (scalars, keep, received, sibling, inverse_third)
    )
    inverses = inverse_third, permute(inverse_third, 1)
    acc, far, panel = kernel_call(
        near_kernel,
        [
            (aval(rows, cols, F32), True),
            (aval(rows, n_far * depth, BF16), True),
            (aval(*panel_first.shape, BF16), True),
        ],
        scalars,
        [loads_first, sibling],
        [inverse_first, panel_first],
        [
            pltpu.VMEM((rows, 2 * depth), BF16),
            pltpu.SemaphoreType.DMA((2 * (rows // row_tile(rows)) + n_far + 1,)),
        ],
        limit=16,
    )
    runs = [(sum(sizes[:i]), n) for i, n in enumerate(sizes)]
    groups = [[run] for run in runs]
    own_second, half_third, half_fourth = kernel_call(
        functools.partial(pack_kernel, groups),
        [(aval(2 * sum(n for _, n in group), half, BF16), True) for group in groups],
        scalars,
        [keep, received],
    )
    x_second = permute(own_second, mask_x)
    by_z2 = permute(half_fourth, mask_z2)
    by_z1 = permute(half_third, mask_z1)
    acc, by_z1, by_z2 = tie((acc, by_z1, by_z2))
    own_third = jnp.concatenate([half_third, by_z1], 0)
    half_fourth = jnp.concatenate([half_fourth, by_z2], 0)
    x_third = permute(own_third, mask_x)
    by_z1 = permute(half_fourth, mask_z1)
    shards, acc, far, panel, own_second, x_second, inverses = tie(
        (shards, acc, far, panel, own_second, x_second, inverses)
    )

    pieces = [v for shard in shards for v in (shard, permute(shard, 1))]
    y_second = [permute(own_second, mask) for mask in y_masks]
    nexts = [inverse_second, panel_second]
    solved_first, keep, send, inverse_second, panel_second = kernel_call(
        functools.partial(far_kernel, n_far, len(nexts)),
        [
            (aval(rows, cols, BF16), False),
            (aval(update_rows, half, F32), True),
            (aval(update_rows, half, BF16), True),
        ]
        + in_vmem(nexts),
        scalars,
        [acc, panel, far, *pieces],
        nexts,
        [
            pltpu.VMEM((rows, cols), BF16),
            pltpu.SemaphoreType.DMA,
            pltpu.SemaphoreType.DMA((len(nexts),)),
        ],
    )
    keep, send, y_second, by_z1, x_third = tie((keep, send, y_second, by_z1, x_third))
    chunks = pair_sum(keep, send, scalars, at_place, column)
    chunks, panel_third = tie((chunks, panel_third))
    panels = panel_third, permute(panel_third, 1)

    def with_x(x_piece, own, y_pieces):
        pieces = [own, x_piece]
        for piece in y_pieces:
            pieces += [piece, permute(piece, mask_x)]
        return pieces

    pieces_second = with_x(x_second, own_second, y_second)
    early = [own_second, x_second, *y_second]
    across_early = [permute(piece, 1) for piece in early]
    own_fourth = jnp.concatenate([half_fourth, by_z1], 0)
    part = reduce_chunks(chunks, column, scalars)
    part, pieces_second, across_early, own_third, own_fourth = tie(
        (part, pieces_second, across_early, own_third, own_fourth)
    )

    def spread(value):
        return lax.all_gather(value, PLANE, axis=0, tiled=True)

    def spread_both(own, sib):
        both = jnp.concatenate([own, sib], 0)
        return [both] + [permute(both, mask) for mask in plane[1:]]

    def plan_of(level, chunk):
        unit = math.gcd(chunk, block)
        places = width, at_place + 1
        if level == 0:
            rows = [divmod(row, block) for row in range(0, update_rows, unit)]
            places = [(child * width + i, row) for child in range(2) for i, row in rows]
        n_next = 4 if level < 2 else 0
        return unit, places, block, at_table[level], at_order[level], 2 * sizes[level], n_pieces, n_next

    n_pieces = len(plane_masks)

    across = across_early[:2]
    for i in range(len(y_masks)):
        across += [across_early[2 + i], permute(pieces_second[3 + 2 * i], 1)]
    pieces_second += across
    mine = spread(part)
    mine, pieces_second, own_third, own_fourth = tie(
        (mine, pieces_second, own_third, own_fourth)
    )
    other = permute(mine, 1)
    x_fourth = permute(own_fourth, mask_x)
    y_third = [permute(own_third, mask) for mask in y_masks]
    solved_second, keep, send, *nexts = solve_whole(
        scalars,
        plan_of(0, part.shape[0]),
        mine,
        other,
        inverse_second,
        panel_second,
        pieces_second,
        [*inverses, *panels],
    )
    keep, send, x_fourth, y_third = tie((keep, send, x_fourth, y_third))

    chunks = pair_sum(keep, send, scalars, at_place + 1, plane)
    chunks, inverse_fourth, panel_fourth = tie((chunks, inverse_fourth, panel_fourth))
    part = reduce_chunks(chunks, plane, scalars)
    part, own_fourth = tie((part, own_fourth))
    sibling = permute(part, mask_z1)
    pieces_third = with_x(x_third, own_third, y_third)
    y_fourth = [permute(own_fourth, mask) for mask in y_masks]
    panel_fourth = panel_fourth.T
    fourth = [
        inverse_fourth, permute(inverse_fourth, 1), panel_fourth, permute(panel_fourth, 1),
    ]
    part, sibling, pieces_third, fourth, y_fourth = tie(
        (part, sibling, pieces_third, fourth, y_fourth)
    )
    parts = spread_both(part, sibling)
    *chunks, keep, send, a, b, c, d = solve_half(
        scalars,
        plan_of(1, part.shape[0]),
        parts,
        nexts[:2],
        nexts[2:],
        pieces_third,
        fourth,
        update_rows,
        at_place + 1,
        plane,
    )
    fourth = [a, b, c, d]
    chunks, keep, send = tie((chunks, keep, send))

    part = reduce_chunks(chunks, plane, scalars)
    part, keep, send = tie((part, keep, send))
    pieces_fourth = with_x(x_fourth, own_fourth, y_fourth)
    halves_third = keep, permute(send, 1)
    part = (part.astype(F32) + permute(part, mask_z1).astype(F32)).astype(BF16)
    sibling = permute(part, mask_z2)
    part, sibling, pieces_fourth, halves_third = tie((part, sibling, pieces_fourth, halves_third))
    parts = spread_both(part, sibling)
    update, keep_fourth, send_fourth = solve_half(
        scalars,
        plan_of(2, part.shape[0]),
        parts,
        fourth[:2],
        fourth[2:],
        pieces_fourth,
        [],
        update_rows,
        0,
        [],
    )
    halves_fourth = keep_fourth, permute(send_fourth, 1)
    everywhere = ("z2", "z1", "x", "y")
    count = lax.axis_size(everywhere)
    arrived = lax.all_to_all(update, everywhere, 0, 0, tiled=True)
    solved_third, solved_fourth = join_columns(scalars, [halves_third, halves_fourth])
    arrived, solved_third, solved_fourth = tie((arrived, solved_third, solved_fourth))
    chunk = update_rows // count
    keep, send = kernel_call(
        functools.partial(core_split_kernel, count),
        [(aval(chunk // 2, half, F32), True)] * 2,
        scalars,
        [arrived],
        scratch=[pltpu.VMEM((chunk, half), F32)],
    )
    ancestor = join_columns(scalars, [(keep, permute(send, 1))])[0]
    return solved_first, solved_second, solved_third, solved_fourth, ancestor


def solution(mesh):
    n_leaf, n_rows = mesh.shape["leaf"], mesh.shape["rows"]
    fine = Mesh(mesh.devices.reshape(n_leaf // 8, 2, 2, 2, n_rows // 2, 2), AXES)
    rows, cols = P(AXES, None), P(None, AXES)
    return jax.shard_map(
        per_device,
        mesh=fine,
        in_specs=(rows,) * 8 + (cols,) * 4 + (P(),) * 3,
        out_specs=(rows,) * 5,
        check_vma=False,
    )
```
